32 devices in a mesh: seq: 16 (over z, y, x), tp: 2 (over core).
Axes of the slice: x: 2, y: 2, z: 4, core: 2. Of those that a mesh axis runs over, the one named last changes fastest.
Arguments:
- query_proj: bfloat16 [4096, 2048], P('tp', 'seq'), may hold values from -6 to 6
- key_proj: bfloat16 [4096, 2048], P('tp', 'seq'), may hold values from -6 to 6
- value_proj: bfloat16 [4096, 2048], P('tp', 'seq'), may hold values from -6 to 6
- short_taps: float32 [3, 3, 4096], P(None, None, 'tp'), may hold values from -3.5 to 3.5
- long_filters: float32 [4096, 2048], P(('tp', 'seq')), may hold values from -2 to 2
- out_weight: bfloat16 [4096, 8192], P('seq', 'tp'), may hold values from -0.09375 to 0.09375
Outputs:
- block_out: bfloat16 [2048, 8192], P('seq', 'tp')
The draws below stay inside these ranges and needn't reach their ends.
All inputs are finite; a program needn't handle non-finite values.
Results may differ from the reference program's by a relative error of at most 0.0058.
Values may be sent and summed in bfloat16 or wider, within the bound.
No kernel may reach another device: no remote copies, remote signals or barrier semaphores. Data moves between devices by JAX's collectives and lax.ppermute only.
A program may use at most 128 MiB of HBM per device.

```python
import jax
import jax.numpy as jnp
from jax import lax

D = 8192
CONV_CHANNELS = 4096
SEQUENCE_LENGTH = 2048


def draw_long_filters(key, part):
    random_splits = jax.random.split(key, 6)
    noisy_component = jax.random.truncated_normal(random_splits[0], -4.0, 4.0, (CONV_CHANNELS, SEQUENCE_LENGTH), jnp.float32)
    slow_share = 0.5
    is_slow = jax.random.uniform(random_splits[1], (CONV_CHANNELS, 1), jnp.float32) < slow_share
    slow_rate = jnp.log(10.0) / SEQUENCE_LENGTH * jnp.exp(jax.random.uniform(random_splits[2], (CONV_CHANNELS, 1), jnp.float32, jnp.log(0.05), jnp.log(0.5)))
    fast_rate = jnp.log(10.0) / jax.random.uniform(random_splits[3], (CONV_CHANNELS, 1), jnp.float32, 30.0, 50.0)
    falloff_speed = jnp.where(is_slow, slow_rate, fast_rate)
    filter_offset = jnp.arange(SEQUENCE_LENGTH, dtype=jnp.float32)[None, :]
    spike_location = jax.random.uniform(random_splits[4], (CONV_CHANNELS, 2), jnp.float32) * SEQUENCE_LENGTH
    spike_retained = jax.random.uniform(random_splits[5], (CONV_CHANNELS, 2), jnp.float32, 0.5, 0.8)
    filter_spikes = jnp.where(filter_offset >= spike_location[:, 0:1], spike_retained[:, 0:1], 1.0) * jnp.where(filter_offset >= spike_location[:, 1:2], spike_retained[:, 1:2], 1.0)
    norm_divisor = jnp.sqrt(2.0 * falloff_speed / (1.0 - jnp.exp(-2.0 * falloff_speed * SEQUENCE_LENGTH)))
    return (noisy_component * jnp.exp(-falloff_speed * filter_offset) * filter_spikes * norm_divisor).astype(jnp.float32)


def level_of(rng, dims, cuts, smallest, largest):
    level, own = 1.0, jax.random.fold_in(rng, 6)
    for dim, shards_of in cuts:
        draws = jnp.exp(jax.random.uniform(jax.random.fold_in(own, dim), (shards_of,), jnp.float32, smallest / len(cuts), largest / len(cuts)))
        level = level * jnp.repeat(draws, dims[dim] // shards_of).reshape([-1 if axis == dim else 1 for axis in range(len(dims))])
    return level


def normal_values(key, shape, deviation, limit, cuts=(), held_as=jnp.bfloat16):
    array = deviation * jax.random.normal(key, shape, jnp.float32)
    if cuts:
        array = array * level_of(key, shape, cuts, -0.22, 0.18)
    return jnp.clip(array, -limit, limit).astype(held_as)


def setup_inputs(seed: int = 0) -> dict:
    keys = jax.random.split(jax.random.key(seed), 7)
    query_proj = normal_values(keys[0], (CONV_CHANNELS, SEQUENCE_LENGTH), 1.0, 6.0, ((0, 2), (1, 16)))
    key_proj = normal_values(keys[1], (CONV_CHANNELS, SEQUENCE_LENGTH), 1.0, 6.0, ((0, 2), (1, 16)))
    value_proj = normal_values(keys[2], (CONV_CHANNELS, SEQUENCE_LENGTH), 1.0, 6.0, ((0, 2), (1, 16)))
    short_taps = normal_values(keys[3], (3, 3, CONV_CHANNELS), 3 ** -0.5, 3.5, ((2, 2),), jnp.float32)
    long_filters = draw_long_filters(jax.random.fold_in(keys[6], 71), 0)
    out_weight = normal_values(keys[5], (CONV_CHANNELS, D), CONV_CHANNELS ** -0.5, 0.09375, ((0, 16), (1, 2)))
    return {"query_proj": query_proj, "key_proj": key_proj, "value_proj": value_proj, "short_taps": short_taps, "long_filters": long_filters, "out_weight": out_weight}


def short_filter(extended, tap_weights):
    return (tap_weights[0][:, None] * extended[:, 2:]
            + tap_weights[1][:, None] * extended[:, 1:-1]
            + tap_weights[2][:, None] * extended[:, :-2])


def convolve_block(block_pair):
    product_block, filter_block = block_pair
    padded_len = 2 * SEQUENCE_LENGTH
    spectrum = jnp.fft.rfft(product_block, n=padded_len, axis=1) * jnp.fft.rfft(filter_block, n=padded_len, axis=1)
    return jnp.fft.irfft(spectrum, n=padded_len, axis=1)[:, :SEQUENCE_LENGTH].astype(product_block.dtype)


def reference(query_proj, key_proj, value_proj, short_taps, long_filters, out_weight):
    shorts = []
    for stream_index, stream in enumerate((query_proj, key_proj, value_proj)):
        extended = jnp.pad(stream.astype(jnp.float32), ((0, 0), (2, 0)))
        shorts.append(short_filter(extended, short_taps[stream_index]))
    query_short, key_short, value_short = shorts
    product = lax.optimization_barrier((key_short * value_short).astype(jnp.bfloat16)).astype(jnp.float32)
    block_rows = 32
    mixed_conv = lax.map(convolve_block, (product.reshape(CONV_CHANNELS // block_rows, block_rows, SEQUENCE_LENGTH),
                                          long_filters.reshape(CONV_CHANNELS // block_rows, block_rows, SEQUENCE_LENGTH)))
    mixed_conv = mixed_conv.reshape(CONV_CHANNELS, SEQUENCE_LENGTH)
    gated_out = (query_short * mixed_conv).astype(jnp.bfloat16)
    result = lax.dot_general(gated_out, out_weight, (((0,), (0,)), ((), ())), preferred_element_type=jnp.float32)
    return result.astype(jnp.bfloat16)
```

```python
import functools
import math

import jax
import jax.numpy as jnp
from jax import lax
from jax.experimental import pallas as pl
from jax.experimental.pallas import tpu as pltpu
from jax.sharding import PartitionSpec as P

PLANE = 4
VMEM_LIMIT = 40 * 2**20


def shifted(value, axis, steps):
    count = lax.axis_size(axis)
    initial, last = (max(0, -steps), min(count, count - steps))
    return lax.ppermute(value, axis, [(source, source + steps) for source in range(initial, last)])


def short_filter(extended, tap_weights):
    return (
        tap_weights[0][:, None] * extended[:, 2:]
        + tap_weights[1][:, None] * extended[:, 1:-1]
        + tap_weights[2][:, None] * extended[:, :-2]
    )


def filtered_streams(streams, taps):
    before = shifted(jnp.stack([stream[:, -2:] for stream in streams]), "seq", 1)
    extended = [
        jnp.concatenate([before[index], stream], axis=1).astype(jnp.float32)
        for index, stream in enumerate(streams)
    ]
    return [short_filter(value, tap) for value, tap in zip(extended, taps)]


def delayed(value, steps, lane, row):
    rolled = pltpu.roll(value, steps, 1)
    above = jnp.where(row >= 1, pltpu.roll(rolled, 1, 0), 0.0)
    return jnp.where(lane >= steps, rolled, above)


def conv_kernel(place_ref, taps_ref, x_ref, h_ref, q_ref, *rest):
    outs, (xpad, gated) = rest[:-2], rest[-2:]
    channels, blocks, width = x_ref.shape
    keep = lax.broadcasted_iota(jnp.int32, (width, width), 1) >= lax.broadcasted_iota(
        jnp.int32, (width, width), 0
    )
    lane = lax.broadcasted_iota(jnp.int32, (blocks, width), 1)
    row = lax.broadcasted_iota(jnp.int32, (blocks, width), 0)
    xpad[:blocks] = jnp.zeros((blocks, width), jnp.float32)

    def one_channel(channel, carry):
        xpad[blocks:] = x_ref[channel].astype(jnp.float32)
        earlier = jnp.zeros((width, width), jnp.float32)
        total = jnp.zeros((blocks, width), jnp.float32)
        bands, shifts = [], []
        for lag in range(blocks):
            rolled = pltpu.roll(
                jnp.broadcast_to(h_ref[channel, lag : lag + 1, :], (width, width)),
                0,
                1,
                stride=1,
                stride_axis=0,
            )
            bands.append(jnp.where(keep, rolled, earlier).astype(jnp.bfloat16))
            earlier = rolled
            shifts.append(xpad[pl.ds(blocks - lag, blocks), :].astype(jnp.bfloat16))
            if len(bands) == 2:
                total += jnp.dot(
                    jnp.concatenate(shifts, axis=1),
                    jnp.concatenate(bands, axis=0),
                    preferred_element_type=jnp.float32,
                )
                bands, shifts = [], []
        query = q_ref[channel].astype(jnp.float32)
        query_short = (
            taps_ref[0, channel] * query
            + taps_ref[1, channel] * delayed(query, 1, lane, row)
            + taps_ref[2, channel] * delayed(query, 2, lane, row)
        )
        gated[pl.ds(pl.multiple_of(channel * blocks, blocks), blocks), :] = query_short * total
        return carry

    lax.fori_loop(0, channels, one_channel, 0, unroll=4)
    inner = len(outs)
    for offset, out in enumerate(outs):
        for outer in range(blocks // inner):
            block = outer * inner + jnp.bitwise_xor(place_ref[0], offset)
            tile = gated[pl.ds(block, channels, stride=blocks), :]
            out[outer] = tile.T.astype(jnp.bfloat16)


def convolve_and_gate(place, taps, product, filters, query, inner):
    channels, blocks, width = product.shape
    vmem = pl.BlockSpec(memory_space=pltpu.VMEM)
    smem = pl.BlockSpec(memory_space=pltpu.SMEM)
    return pl.pallas_call(
        conv_kernel,
        out_shape=[jax.ShapeDtypeStruct((blocks // inner, width, channels), jnp.bfloat16)] * inner,
        in_specs=[smem, smem, vmem, vmem, vmem],
        out_specs=[vmem] * inner,
        scratch_shapes=[
            pltpu.VMEM((2 * blocks, width), jnp.float32),
            pltpu.VMEM((channels * blocks, width), jnp.float32),
        ],
        compiler_params=pltpu.CompilerParams(vmem_limit_bytes=VMEM_LIMIT),
        cost_estimate=pl.CostEstimate(
            flops=2 * channels * width * width * blocks * blocks,
            bytes_accessed=12 * channels * blocks * width,
            transcendentals=0,
        ),
    )(place, taps, product, filters, query)


def project_kernel(pieces, place_ref, *refs):
    gates, weights, outs = refs[: 8 * pieces], refs[8 * pieces : -pieces], refs[-pieces:]
    tiles = [ref[...] for ref in weights[:3]] + [
        jnp.concatenate([weights[3][...], weights[4][...]], axis=0)
    ]
    depth = tiles[0].shape[0] // 2
    for piece in range(pieces):
        mine = [ref[...].reshape(-1, depth) for ref in gates[8 * piece : 8 * piece + 8]]
        total = None
        for index, tile in enumerate(tiles):
            left = jnp.concatenate([mine[2 * index], mine[2 * index + 1]], axis=1)
            term = jnp.dot(left, tile, preferred_element_type=jnp.float32)
            total = term if total is None else total + term
        outs[piece][...] = total.astype(outs[piece].dtype)


def project(place, gates, weights, steps, dtype, tile=512):
    _, _, planes, rows, depth = gates.shape
    columns = weights[0].shape[1]

    def gate_spec(step, offset, half):
        def index(column, place_ref):
            inner, outer, core = place_ref[0], place_ref[1], place_ref[2]
            owner = inner ^ offset
            source = 2 * (owner % 2) + half
            return ((owner // 2) ^ core, source ^ inner, (outer + step) % planes, 0, 0)

        return pl.BlockSpec((1, 1, 1, rows, depth), index)

    gate_specs = [
        gate_spec(step, offset, half) for step in steps for offset in range(PLANE) for half in range(2)
    ]
    weight_specs = [
        pl.BlockSpec((weight.shape[0], tile), lambda column, place_ref: (0, column))
        for weight in weights
    ]
    return pl.pallas_call(
        functools.partial(project_kernel, len(steps)),
        out_shape=[jax.ShapeDtypeStruct((rows, columns), dtype)] * len(steps),
        grid_spec=pltpu.PrefetchScalarGridSpec(
            num_scalar_prefetch=1,
            grid=(columns // tile,),
            in_specs=gate_specs + weight_specs,
            out_specs=[pl.BlockSpec((rows, tile), lambda column, place_ref: (0, column))] * len(steps),
        ),
        compiler_params=pltpu.CompilerParams(vmem_limit_bytes=VMEM_LIMIT),
        cost_estimate=pl.CostEstimate(
            flops=2 * len(steps) * rows * 8 * depth * columns,
            bytes_accessed=16 * depth * columns + 4 * len(steps) * rows * columns,
            transcendentals=0,
        ),
    )(place, *[gates] * len(gate_specs), *weights)


def by_planes(query_proj, key_proj, value_proj, short_taps, long_filters, out_weight):
    seq_count, tp_count = lax.axis_size("seq"), lax.axis_size("tp")
    planes = seq_count // PLANE
    place_seq, core = lax.axis_index("seq"), lax.axis_index("tp")
    inner, outer = place_seq % PLANE, place_seq // PLANE
    place = jnp.stack([inner, outer, core]).astype(jnp.int32)
    channels, width = long_filters.shape[0], query_proj.shape[1]

    across = [(source, source ^ 1) for source in range(seq_count)]
    along = [(source, source ^ 2) for source in range(seq_count)]
    up = [(source, (source + PLANE) % seq_count) for source in range(seq_count)]
    down = [(target, source) for source, target in up]

    def spread(stream):
        parts = lax.all_to_all(
            stream.reshape(seq_count, channels, width), "seq", split_axis=0, concat_axis=0, tiled=True
        )
        return parts.transpose(1, 0, 2)

    weight_x = lax.ppermute(out_weight, "seq", across)
    weight_y = lax.ppermute(out_weight, "seq", along)
    half_rows = out_weight.shape[0] // 2
    weight_top = lax.ppermute(weight_y[:half_rows], "seq", across)
    weight_end = lax.ppermute(weight_x[half_rows:], "seq", along)
    weights = [out_weight, weight_x, weight_y, weight_top, weight_end]

    query = spread(query_proj)
    key_short, value_short = filtered_streams((key_proj, value_proj), short_taps[1:])
    product = spread((key_short * value_short).astype(jnp.bfloat16))
    taps = lax.dynamic_slice_in_dim(short_taps[0], place_seq * channels, channels, axis=1)
    filters = long_filters.reshape(channels, seq_count, width)
    gated = convolve_and_gate(place, taps, product, filters, query, PLANE)

    landed = []
    for offset, message in enumerate(gated):
        pairs = []
        for source in range(seq_count):
            z, q = divmod(source, PLANE)
            for tp in range(tp_count):
                target = (planes // tp_count * tp + z // tp_count) * PLANE + (q ^ offset)
                pairs.append((source * tp_count + tp, target * tp_count + z % tp_count))
        landed.append(lax.ppermute(message, ("seq", "tp"), pairs))
    own = jnp.stack(landed)
    other = lax.ppermute(own, "tp", [(0, 1), (1, 0)])
    gates = jnp.stack([own, other])

    (far,) = project(place, gates, weights, (2,), jnp.bfloat16)
    half = far.shape[1] // 2
    far_left = lax.ppermute(far[:, :half], "seq", up)
    far_right = lax.ppermute(far[:, half:], "seq", down)
    ahead, behind = project(place, gates, weights, (1, planes - 1), jnp.bfloat16)
    near_right = lax.ppermute(ahead[:, half:], "seq", up)
    near_left = lax.ppermute(behind[:, :half], "seq", down)
    (mine,) = project(place, gates, weights, (0,), jnp.float32)

    def added(first, second):
        return (first.astype(jnp.float32) + second.astype(jnp.float32)).astype(jnp.bfloat16)

    sum_left = lax.ppermute(added(ahead[:, :half], far_left), "seq", up)
    sum_right = lax.ppermute(added(behind[:, half:], far_right), "seq", down)
    left = mine[:, :half] + near_left.astype(jnp.float32) + sum_left.astype(jnp.float32)
    right = mine[:, half:] + near_right.astype(jnp.float32) + sum_right.astype(jnp.float32)
    return jnp.concatenate([left, right], axis=1).astype(jnp.bfloat16)


PRECISE = lax.Precision.HIGHEST


def phase_table(period, out_size, in_size, direction):
    out_index = lax.broadcasted_iota(jnp.int32, (out_size, in_size), 0)
    in_index = lax.broadcasted_iota(jnp.int32, (out_size, in_size), 1)
    phase_angle = (out_index * in_index % period).astype(jnp.float32) * (
        direction * 2.0 * math.pi / period
    )
    return (jnp.cos(phase_angle), jnp.sin(phase_angle))


def left_apply(phase, signal):
    return jnp.einsum("kn,cnm->ckm", phase, signal, precision=PRECISE)


def right_apply(signal, phase):
    return jnp.einsum("ckn,nm->ckm", signal, phase, precision=PRECISE)


def forward_spectrum(signal, inner_size):
    channels_here, length = signal.shape
    period = 2 * length
    outer_size = period // inner_size
    blocks = signal.reshape(channels_here, outer_size // 2, inner_size)
    left_re, left_im = phase_table(outer_size, outer_size, outer_size // 2, -1.0)
    section_re = left_apply(left_re, blocks)
    section_im = left_apply(left_im, blocks)
    twist_re, twist_im = phase_table(period, outer_size, inner_size, -1.0)
    turned_re = section_re * twist_re - section_im * twist_im
    turned_im = section_re * twist_im + section_im * twist_re
    right_re, right_im = phase_table(inner_size, inner_size, inner_size, -1.0)
    spec_re = right_apply(turned_re, right_re) - right_apply(turned_im, right_im)
    spec_im = right_apply(turned_re, right_im) + right_apply(turned_im, right_re)
    return (spec_re, spec_im)


def inverse_signal(spec_re, spec_im, length, inner_size):
    channels_here = spec_re.shape[0]
    period = 2 * length
    outer_size = period // inner_size
    right_re, right_im = phase_table(inner_size, inner_size, inner_size, 1.0)
    mid_re = right_apply(spec_re, right_re) - right_apply(spec_im, right_im)
    mid_im = right_apply(spec_re, right_im) + right_apply(spec_im, right_re)
    twist_re, twist_im = phase_table(period, outer_size, inner_size, 1.0)
    turned_re = mid_re * twist_re - mid_im * twist_im
    turned_im = mid_re * twist_im + mid_im * twist_re
    left_re, left_im = phase_table(outer_size, outer_size // 2, outer_size, 1.0)
    signal = left_apply(left_re, turned_re) - left_apply(left_im, turned_im)
    return signal.reshape(channels_here, length) / period


def long_convolve(signal, filters, inner_size):
    length = signal.shape[1]
    data_re, data_im = forward_spectrum(signal, inner_size)
    filt_re, filt_im = forward_spectrum(filters, inner_size)
    prod_re = data_re * filt_re - data_im * filt_im
    prod_im = data_re * filt_im + data_im * filt_re
    return inverse_signal(prod_re, prod_im, length, inner_size)


def by_whole_rows(query_proj, key_proj, value_proj, short_taps, long_filters, out_weight):
    inner_size = query_proj.shape[1] // 2
    query_short, key_short, value_short = filtered_streams(
        (query_proj, key_proj, value_proj), short_taps
    )
    product = (key_short * value_short).astype(jnp.bfloat16)
    spread = lax.all_to_all(product, "seq", split_axis=0, concat_axis=1, tiled=True)
    mixed_conv = long_convolve(spread.astype(jnp.float32), long_filters, inner_size)
    returned = lax.all_to_all(mixed_conv, "seq", split_axis=1, concat_axis=0, tiled=True)
    gated_out = (query_short * returned).astype(jnp.bfloat16)
    result = lax.dot_general(
        lax.all_gather(gated_out, "tp", axis=0, tiled=True),
        lax.all_gather(out_weight, "seq", axis=0, tiled=True),
        (((0,), (0,)), ((), ())),
        preferred_element_type=jnp.float32,
    )
    return result.astype(jnp.bfloat16)


def solution(mesh):
    planes, cores = mesh.shape["seq"] // PLANE, mesh.shape["tp"]
    plan = by_planes if planes == PLANE and cores == 2 else by_whole_rows
    return jax.shard_map(
        plan,
        mesh=mesh,
        in_specs=(
            P("tp", "seq"),
            P("tp", "seq"),
            P("tp", "seq"),
            P(None, None, "tp"),
            P(("tp", "seq"), None),
            P("seq", "tp"),
        ),
        out_specs=P("seq", "tp"),
        check_vma=False,
    )
```

```python
import functools
import math

import jax
import jax.numpy as jnp
from jax import lax
from jax.experimental import pallas as pl
from jax.experimental.pallas import tpu as pltpu
from jax.sharding import PartitionSpec as P

PLANE = 4
VMEM_LIMIT = 40 * 2**20


def shifted(value, axis, steps):
    count = lax.axis_size(axis)
    initial, last = (max(0, -steps), min(count, count - steps))
    return lax.ppermute(value, axis, [(source, source + steps) for source in range(initial, last)])


def short_filter(extended, tap_weights):
    return (
        tap_weights[0][:, None] * extended[:, 2:]
        + tap_weights[1][:, None] * extended[:, 1:-1]
        + tap_weights[2][:, None] * extended[:, :-2]
    )


def filtered_streams(streams, taps):
    before = shifted(jnp.stack([stream[:, -2:] for stream in streams]), "seq", 1)
    extended = [
        jnp.concatenate([before[index], stream], axis=1).astype(jnp.float32)
        for index, stream in enumerate(streams)
    ]
    return [short_filter(value, tap) for value, tap in zip(extended, taps)]


def delayed(value, steps, lane, row):
    rolled = pltpu.roll(value, steps, 1)
    above = jnp.where(row >= 1, pltpu.roll(rolled, 1, 0), 0.0)
    return jnp.where(lane >= steps, rolled, above)


def conv_kernel(place_ref, taps_ref, x_ref, h_ref, q_ref, *rest):
    outs, (xpad, gated) = rest[:-2], rest[-2:]
    channels, blocks, width = x_ref.shape
    keep = lax.broadcasted_iota(jnp.int32, (width, width), 1) >= lax.broadcasted_iota(
        jnp.int32, (width, width), 0
    )
    lane = lax.broadcasted_iota(jnp.int32, (blocks, width), 1)
    row = lax.broadcasted_iota(jnp.int32, (blocks, width), 0)
    xpad[:blocks] = jnp.zeros((blocks, width), jnp.float32)

    def one_channel(channel, carry):
        xpad[blocks:] = x_ref[channel].astype(jnp.float32)
        earlier = jnp.zeros((width, width), jnp.float32)
        total = jnp.zeros((blocks, width), jnp.float32)
        bands, shifts = [], []
        for lag in range(blocks):
            rolled = pltpu.roll(
                jnp.broadcast_to(h_ref[channel, lag : lag + 1, :], (width, width)),
                0,
                1,
                stride=1,
                stride_axis=0,
            )
            bands.append(jnp.where(keep, rolled, earlier).astype(jnp.bfloat16))
            earlier = rolled
            shifts.append(xpad[pl.ds(blocks - lag, blocks), :].astype(jnp.bfloat16))
            if len(bands) == 2:
                total += jnp.dot(
                    jnp.concatenate(shifts, axis=1),
                    jnp.concatenate(bands, axis=0),
                    preferred_element_type=jnp.float32,
                )
                bands, shifts = [], []
        query = q_ref[channel].astype(jnp.float32)
        query_short = (
            taps_ref[0, channel] * query
            + taps_ref[1, channel] * delayed(query, 1, lane, row)
            + taps_ref[2, channel] * delayed(query, 2, lane, row)
        )
        gated[pl.ds(pl.multiple_of(channel * blocks, blocks), blocks), :] = query_short * total
        return carry

    lax.fori_loop(0, channels, one_channel, 0, unroll=4)
    inner = len(outs)
    for offset, out in enumerate(outs):
        for outer in range(blocks // inner):
            block = outer * inner + jnp.bitwise_xor(place_ref[0], offset)
            tile = gated[pl.ds(block, channels, stride=blocks), :]
            out[outer] = tile.T.astype(jnp.bfloat16)


def convolve_and_gate(place, taps, product, filters, query, inner):
    channels, blocks, width = product.shape
    vmem = pl.BlockSpec(memory_space=pltpu.VMEM)
    smem = pl.BlockSpec(memory_space=pltpu.SMEM)
    return pl.pallas_call(
        conv_kernel,
        out_shape=[jax.ShapeDtypeStruct((blocks // inner, width, channels), jnp.bfloat16)] * inner,
        in_specs=[smem, smem, vmem, vmem, vmem],
        out_specs=[vmem] * inner,
        scratch_shapes=[
            pltpu.VMEM((2 * blocks, width), jnp.float32),
            pltpu.VMEM((channels * blocks, width), jnp.float32),
        ],
        compiler_params=pltpu.CompilerParams(vmem_limit_bytes=VMEM_LIMIT),
        cost_estimate=pl.CostEstimate(
            flops=2 * channels * width * width * blocks * blocks,
            bytes_accessed=12 * channels * blocks * width,
            transcendentals=0,
        ),
    )(place, taps, product, filters, query)


def project_kernel(pieces, place_ref, *refs):
    gates, weight, outs = refs[: 8 * pieces], refs[8 * pieces], refs[-pieces:]
    depth = weight.shape[0] // 8
    for piece in range(pieces):
        mine = [ref[...].reshape(-1, depth) for ref in gates[8 * piece : 8 * piece + 8]]
        total = jnp.dot(
            jnp.concatenate(mine, axis=1), weight[...], preferred_element_type=jnp.float32
        )
        outs[piece][...] = total.astype(outs[piece].dtype)


def project(place, gates, weight, steps, dtype, tile=512):
    _, _, planes, rows, depth = gates.shape
    columns = weight.shape[1]

    def gate_spec(step, owner, half):
        def index(column, place_ref):
            inner, outer, core = place_ref[0], place_ref[1], place_ref[2]
            source = 2 * (owner % 2) + half
            return ((owner // 2) ^ core, source ^ inner, (outer + step) % planes, 0, 0)

        return pl.BlockSpec((1, 1, 1, rows, depth), index)

    gate_specs = [
        gate_spec(step, owner, half) for step in steps for owner in range(PLANE) for half in range(2)
    ]
    weight_spec = pl.BlockSpec((weight.shape[0], tile), lambda column, place_ref: (0, column))
    return pl.pallas_call(
        functools.partial(project_kernel, len(steps)),
        out_shape=[jax.ShapeDtypeStruct((rows, columns), dtype)] * len(steps),
        grid_spec=pltpu.PrefetchScalarGridSpec(
            num_scalar_prefetch=1,
            grid=(columns // tile,),
            in_specs=gate_specs + [weight_spec],
            out_specs=[pl.BlockSpec((rows, tile), lambda column, place_ref: (0, column))] * len(steps),
        ),
        compiler_params=pltpu.CompilerParams(vmem_limit_bytes=VMEM_LIMIT),
        cost_estimate=pl.CostEstimate(
            flops=2 * len(steps) * rows * 8 * depth * columns,
            bytes_accessed=16 * depth * columns + 4 * len(steps) * rows * columns,
            transcendentals=0,
        ),
    )(place, *[gates] * len(gate_specs), weight)


def by_planes(query_proj, key_proj, value_proj, short_taps, long_filters, out_weight):
    seq_count, tp_count = lax.axis_size("seq"), lax.axis_size("tp")
    planes = seq_count // PLANE
    place_seq, core = lax.axis_index("seq"), lax.axis_index("tp")
    inner, outer = place_seq % PLANE, place_seq // PLANE
    place = jnp.stack([inner, outer, core]).astype(jnp.int32)
    channels, width = long_filters.shape[0], query_proj.shape[1]

    up = [(source, (source + PLANE) % seq_count) for source in range(seq_count)]
    down = [(target, source) for source, target in up]

    def spread(stream):
        parts = lax.all_to_all(
            stream.reshape(seq_count, channels, width), "seq", split_axis=0, concat_axis=0, tiled=True
        )
        return parts.transpose(1, 0, 2)

    groups = [list(range(first, first + PLANE)) for first in range(0, seq_count, PLANE)]
    weight = lax.all_gather(out_weight, "seq", axis=0, tiled=True, axis_index_groups=groups)

    query = spread(query_proj)
    key_short, value_short = filtered_streams((key_proj, value_proj), short_taps[1:])
    product = spread((key_short * value_short).astype(jnp.bfloat16))
    taps = lax.dynamic_slice_in_dim(short_taps[0], place_seq * channels, channels, axis=1)
    filters = long_filters.reshape(channels, seq_count, width)
    gated = convolve_and_gate(place, taps, product, filters, query, PLANE)

    landed = []
    for offset, message in enumerate(gated):
        pairs = []
        for source in range(seq_count):
            z, q = divmod(source, PLANE)
            for tp in range(tp_count):
                target = (planes // tp_count * tp + z // tp_count) * PLANE + (q ^ offset)
                pairs.append((source * tp_count + tp, target * tp_count + z % tp_count))
        landed.append(lax.ppermute(message, ("seq", "tp"), pairs))
    own = jnp.stack(landed)
    other = lax.ppermute(own, "tp", [(0, 1), (1, 0)])
    gates = jnp.stack([own, other])

    (far,) = project(place, gates, weight, (2,), jnp.bfloat16)
    half = far.shape[1] // 2
    far_left = lax.ppermute(far[:, :half], "seq", up)
    far_right = lax.ppermute(far[:, half:], "seq", down)
    ahead, behind = project(place, gates, weight, (1, planes - 1), jnp.bfloat16)
    near_right = lax.ppermute(ahead[:, half:], "seq", up)
    near_left = lax.ppermute(behind[:, :half], "seq", down)
    (mine,) = project(place, gates, weight, (0,), jnp.float32)

    def added(first, second):
        return (first.astype(jnp.float32) + second.astype(jnp.float32)).astype(jnp.bfloat16)

    sum_left = lax.ppermute(added(ahead[:, :half], far_left), "seq", up)
    sum_right = lax.ppermute(added(behind[:, half:], far_right), "seq", down)
    left = mine[:, :half] + near_left.astype(jnp.float32) + sum_left.astype(jnp.float32)
    right = mine[:, half:] + near_right.astype(jnp.float32) + sum_right.astype(jnp.float32)
    return jnp.concatenate([left, right], axis=1).astype(jnp.bfloat16)


PRECISE = lax.Precision.HIGHEST


def phase_table(period, out_size, in_size, direction):
    out_index = lax.broadcasted_iota(jnp.int32, (out_size, in_size), 0)
    in_index = lax.broadcasted_iota(jnp.int32, (out_size, in_size), 1)
    phase_angle = (out_index * in_index % period).astype(jnp.float32) * (
        direction * 2.0 * math.pi / period
    )
    return (jnp.cos(phase_angle), jnp.sin(phase_angle))


def left_apply(phase, signal):
    return jnp.einsum("kn,cnm->ckm", phase, signal, precision=PRECISE)


def right_apply(signal, phase):
    return jnp.einsum("ckn,nm->ckm", signal, phase, precision=PRECISE)


def forward_spectrum(signal, inner_size):
    channels_here, length = signal.shape
    period = 2 * length
    outer_size = period // inner_size
    blocks = signal.reshape(channels_here, outer_size // 2, inner_size)
    left_re, left_im = phase_table(outer_size, outer_size, outer_size // 2, -1.0)
    section_re = left_apply(left_re, blocks)
    section_im = left_apply(left_im, blocks)
    twist_re, twist_im = phase_table(period, outer_size, inner_size, -1.0)
    turned_re = section_re * twist_re - section_im * twist_im
    turned_im = section_re * twist_im + section_im * twist_re
    right_re, right_im = phase_table(inner_size, inner_size, inner_size, -1.0)
    spec_re = right_apply(turned_re, right_re) - right_apply(turned_im, right_im)
    spec_im = right_apply(turned_re, right_im) + right_apply(turned_im, right_re)
    return (spec_re, spec_im)


def inverse_signal(spec_re, spec_im, length, inner_size):
    channels_here = spec_re.shape[0]
    period = 2 * length
    outer_size = period // inner_size
    right_re, right_im = phase_table(inner_size, inner_size, inner_size, 1.0)
    mid_re = right_apply(spec_re, right_re) - right_apply(spec_im, right_im)
    mid_im = right_apply(spec_re, right_im) + right_apply(spec_im, right_re)
    twist_re, twist_im = phase_table(period, outer_size, inner_size, 1.0)
    turned_re = mid_re * twist_re - mid_im * twist_im
    turned_im = mid_re * twist_im + mid_im * twist_re
    left_re, left_im = phase_table(outer_size, outer_size // 2, outer_size, 1.0)
    signal = left_apply(left_re, turned_re) - left_apply(left_im, turned_im)
    return signal.reshape(channels_here, length) / period


def long_convolve(signal, filters, inner_size):
    length = signal.shape[1]
    data_re, data_im = forward_spectrum(signal, inner_size)
    filt_re, filt_im = forward_spectrum(filters, inner_size)
    prod_re = data_re * filt_re - data_im * filt_im
    prod_im = data_re * filt_im + data_im * filt_re
    return inverse_signal(prod_re, prod_im, length, inner_size)


def by_whole_rows(query_proj, key_proj, value_proj, short_taps, long_filters, out_weight):
    inner_size = query_proj.shape[1] // 2
    query_short, key_short, value_short = filtered_streams(
        (query_proj, key_proj, value_proj), short_taps
    )
    product = (key_short * value_short).astype(jnp.bfloat16)
    spread = lax.all_to_all(product, "seq", split_axis=0, concat_axis=1, tiled=True)
    mixed_conv = long_convolve(spread.astype(jnp.float32), long_filters, inner_size)
    returned = lax.all_to_all(mixed_conv, "seq", split_axis=1, concat_axis=0, tiled=True)
    gated_out = (query_short * returned).astype(jnp.bfloat16)
    result = lax.dot_general(
        lax.all_gather(gated_out, "tp", axis=0, tiled=True),
        lax.all_gather(out_weight, "seq", axis=0, tiled=True),
        (((0,), (0,)), ((), ())),
        preferred_element_type=jnp.float32,
    )
    return result.astype(jnp.bfloat16)


def solution(mesh):
    planes, cores = mesh.shape["seq"] // PLANE, mesh.shape["tp"]
    plan = by_planes if planes == PLANE and cores == 2 else by_whole_rows
    return jax.shard_map(
        plan,
        mesh=mesh,
        in_specs=(
            P("tp", "seq"),
            P("tp", "seq"),
            P("tp", "seq"),
            P(None, None, "tp"),
            P(("tp", "seq"), None),
            P("seq", "tp"),
        ),
        out_specs=P("seq", "tp"),
        check_vma=False,
    )
```

```python
import functools
import math

import jax
import jax.numpy as jnp
from jax import lax
from jax.experimental import pallas as pl
from jax.experimental.pallas import tpu as pltpu
from jax.sharding import PartitionSpec as P

EARLY_EIGHTHS = 5
PLANE = 4
VMEM_LIMIT = 40 * 2**20


def shifted(value, axis, steps):
    count = lax.axis_size(axis)
    initial, last = (max(0, -steps), min(count, count - steps))
    return lax.ppermute(value, axis, [(source, source + steps) for source in range(initial, last)])


def short_filter(extended, tap_weights):
    return (
        tap_weights[0][:, None] * extended[:, 2:]
        + tap_weights[1][:, None] * extended[:, 1:-1]
        + tap_weights[2][:, None] * extended[:, :-2]
    )


def last_positions(streams):
    return jnp.stack([stream[:, -2:] for stream in streams])


def filtered_streams(streams, tails, taps):
    before = shifted(tails, "seq", 1)
    extended = [
        jnp.concatenate([before[index], stream], axis=1).astype(jnp.float32)
        for index, stream in enumerate(streams)
    ]
    return [short_filter(value, tap) for value, tap in zip(extended, taps)]


BAND = 32
GROUP = 8


def conv_kernel(x_ref, h_ref, y_ref, shifted_x):
    channels, blocks, width = x_ref.shape
    parts = width // BAND
    band_lane = lax.broadcasted_iota(jnp.int32, (BAND, width), 1)
    keep = band_lane > lax.broadcasted_iota(jnp.int32, (BAND, width), 0)
    lane = lax.broadcasted_iota(jnp.int32, (blocks, width), 1)
    row = lax.broadcasted_iota(jnp.int32, (blocks, width), 0)
    shifted_x[...] = jnp.zeros(shifted_x.shape, jnp.float32)

    def one_channel(slot, channel):
        signal = x_ref[channel].astype(jnp.float32)
        shifted_x[slot, 0, blocks : 2 * blocks] = signal
        for part in range(1, parts):
            left = width - BAND * part
            turned = pltpu.roll(signal, left, 1)
            following = jnp.where(row == blocks - 1, 0.0, pltpu.roll(turned, blocks - 1, 0))
            shifted_x[slot, part, blocks : 2 * blocks] = jnp.where(lane < left, turned, following)
            shifted_x[slot, part, blocks - 8 : blocks] = jnp.where(
                (lane[:8] >= left) & (row[:8] == 7), jnp.broadcast_to(turned[:1], (8, width)), 0.0
            )
        earlier = jnp.zeros((BAND, width), jnp.float32)
        bands, signals = [], []
        for lag in range(blocks + 1):
            delayed_filter = jnp.zeros((BAND, width), jnp.float32)
            if lag < blocks:
                delayed_filter = pltpu.roll(
                    jnp.broadcast_to(h_ref[channel, lag : lag + 1, :], (BAND, width)),
                    1,
                    1,
                    stride=1,
                    stride_axis=0,
                )
            bands.append(jnp.where(keep, delayed_filter, earlier).astype(jnp.bfloat16))
            earlier = delayed_filter
            ahead = [shifted_x[slot, part, lag : lag + blocks, :] for part in range(parts)]
            signals.append(jnp.concatenate(ahead, axis=0).astype(jnp.bfloat16))
        total = lax.dot_general(
            jnp.concatenate(signals, axis=1),
            jnp.concatenate(bands, axis=1),
            (((1,), (1,)), ((), ())),
            preferred_element_type=jnp.float32,
        )
        y_ref[channel] = jnp.concatenate(
            [total[part * blocks : (part + 1) * blocks] for part in range(parts)], axis=1
        )

    def one_group(group, carry):
        for slot in range(GROUP):
            one_channel(slot, group * GROUP + slot)
        return carry

    lax.fori_loop(0, channels // GROUP, one_group, 0)


VMEM = pl.BlockSpec(memory_space=pltpu.VMEM)
SMEM = pl.BlockSpec(memory_space=pltpu.SMEM)


def convolve(product, filters):
    channels, blocks, width = product.shape
    return pl.pallas_call(
        conv_kernel,
        out_shape=jax.ShapeDtypeStruct(product.shape, jnp.float32),
        in_specs=[VMEM, VMEM],
        out_specs=VMEM,
        scratch_shapes=[pltpu.VMEM((GROUP, width // BAND, 2 * blocks + 8, width), jnp.float32)],
        compiler_params=pltpu.CompilerParams(vmem_limit_bytes=VMEM_LIMIT),
        cost_estimate=pl.CostEstimate(
            flops=16 * channels * width * width * blocks * blocks,
            bytes_accessed=10 * channels * blocks * width,
            transcendentals=0,
        ),
    )(product, filters)


def delayed(value, steps, lane, row):
    rolled = pltpu.roll(value, steps, 1)
    above = jnp.where(row >= 1, pltpu.roll(rolled, 1, 0), 0.0)
    return jnp.where(lane >= steps, rolled, above)


def gate_kernel(place_ref, taps_ref, q_ref, y_ref, *rest):
    outs, gated = rest[:-1], rest[-1]
    channels, blocks, width = y_ref.shape
    lane = lax.broadcasted_iota(jnp.int32, (blocks, width), 1)
    row = lax.broadcasted_iota(jnp.int32, (blocks, width), 0)

    def one_channel(channel, carry):
        query = q_ref[channel].astype(jnp.float32)
        query_short = (
            taps_ref[0, channel] * query
            + taps_ref[1, channel] * delayed(query, 1, lane, row)
            + taps_ref[2, channel] * delayed(query, 2, lane, row)
        )
        gated[pl.ds(pl.multiple_of(channel * blocks, blocks), blocks), :] = query_short * y_ref[channel]
        return carry

    lax.fori_loop(0, channels, one_channel, 0, unroll=8)
    inner = len(outs)
    for offset, out in enumerate(outs):
        for outer in range(blocks // inner):
            block = outer * inner + jnp.bitwise_xor(place_ref[0], offset)
            tile = gated[pl.ds(block, channels, stride=blocks), :]
            out[outer] = tile.T.astype(jnp.bfloat16)


def gate(place, taps, query, mixed, inner):
    channels, blocks, width = mixed.shape
    return pl.pallas_call(
        gate_kernel,
        out_shape=[jax.ShapeDtypeStruct((blocks // inner, width, channels), jnp.bfloat16)] * inner,
        in_specs=[SMEM, SMEM, VMEM, VMEM],
        out_specs=[VMEM] * inner,
        scratch_shapes=[pltpu.VMEM((channels * blocks, width), jnp.float32)],
        compiler_params=pltpu.CompilerParams(vmem_limit_bytes=VMEM_LIMIT),
        cost_estimate=pl.CostEstimate(
            flops=40 * channels * width * blocks,
            bytes_accessed=8 * channels * blocks * width,
            transcendentals=0,
        ),
    )(place, taps, query, mixed)


def project_kernel(pieces, place_ref, *refs):
    gates, weights, outs = refs[: 8 * pieces], refs[8 * pieces : -pieces], refs[-pieces:]
    depth = gates[0].shape[-1]
    for piece in range(pieces):
        mine = [ref[...].reshape(-1, depth) for ref in gates[8 * piece : 8 * piece + 8]]
        total, taken = None, 0
        for weight in weights:
            count = weight.shape[0] // depth
            left = jnp.concatenate(mine[taken : taken + count], axis=1)
            term = jnp.dot(left, weight[...], preferred_element_type=jnp.float32)
            total = term if total is None else total + term
            taken += count
        outs[piece][...] = total.astype(outs[piece].dtype)


def project(place, gates, weights, steps, dtype, tile=512):
    _, _, planes, rows, depth = gates.shape
    columns = weights[0].shape[1]
    ordered = len(weights) == 1

    def gate_spec(step, offset, half):
        def index(column, place_ref):
            inner, outer, core = place_ref[0], place_ref[1], place_ref[2]
            owner = offset if ordered else inner ^ offset
            source = 2 * (owner % 2) + half
            return ((owner // 2) ^ core, source ^ inner, (outer + step) % planes, 0, 0)

        return pl.BlockSpec((1, 1, 1, rows, depth), index)

    gate_specs = [
        gate_spec(step, offset, half) for step in steps for offset in range(PLANE) for half in range(2)
    ]
    weight_specs = [
        pl.BlockSpec((weight.shape[0], tile), lambda column, place_ref: (0, column))
        for weight in weights
    ]
    return pl.pallas_call(
        functools.partial(project_kernel, len(steps)),
        out_shape=[jax.ShapeDtypeStruct((rows, columns), dtype)] * len(steps),
        grid_spec=pltpu.PrefetchScalarGridSpec(
            num_scalar_prefetch=1,
            grid=(columns // tile,),
            in_specs=gate_specs + weight_specs,
            out_specs=[pl.BlockSpec((rows, tile), lambda column, place_ref: (0, column))] * len(steps),
        ),
        compiler_params=pltpu.CompilerParams(vmem_limit_bytes=VMEM_LIMIT),
        cost_estimate=pl.CostEstimate(
            flops=2 * len(steps) * rows * 8 * depth * columns,
            bytes_accessed=16 * depth * columns + 4 * len(steps) * rows * columns,
            transcendentals=0,
        ),
    )(place, *[gates] * len(gate_specs), *weights)


def by_planes(query_proj, key_proj, value_proj, short_taps, long_filters, out_weight):
    seq_count, tp_count = lax.axis_size("seq"), lax.axis_size("tp")
    planes = seq_count // PLANE
    place_seq, core = lax.axis_index("seq"), lax.axis_index("tp")
    inner, outer = place_seq % PLANE, place_seq // PLANE
    place = jnp.stack([inner, outer, core]).astype(jnp.int32)
    channels, width = long_filters.shape[0], query_proj.shape[1]

    up = [(source, (source + PLANE) % seq_count) for source in range(seq_count)]
    down = [(target, source) for source, target in up]

    def spread(stream):
        parts = lax.all_to_all(
            stream.reshape(seq_count, channels, width), "seq", split_axis=0, concat_axis=0, tiled=True
        )
        return parts.transpose(1, 0, 2)

    in_plane = [
        [(source, source ^ offset) for source in range(seq_count)] for offset in range(PLANE)
    ]
    groups = [list(range(first, first + PLANE)) for first in range(0, seq_count, PLANE)]
    tails = last_positions((key_proj, value_proj))
    tails, out_weight = lax.optimization_barrier((tails, out_weight))
    early = out_weight.shape[1] * EARLY_EIGHTHS // 8
    weight_early = lax.all_gather(
        out_weight[:, :early], "seq", axis=0, tiled=True, axis_index_groups=groups
    )
    key_short, value_short = filtered_streams((key_proj, value_proj), tails, short_taps[1:])
    product = spread((key_short * value_short).astype(jnp.bfloat16))
    query_proj, product = lax.optimization_barrier((query_proj, product))
    query = spread(query_proj)
    taps = lax.dynamic_slice_in_dim(short_taps[0], place_seq * channels, channels, axis=1)
    filters = long_filters[:, ::-1].reshape(channels, seq_count, width)
    gated = gate(place, taps, query, convolve(product, filters), PLANE)

    landed = []
    for offset, message in enumerate(gated):
        pairs = []
        for source in range(seq_count):
            z, q = divmod(source, PLANE)
            for tp in range(tp_count):
                target = (planes // tp_count * tp + z // tp_count) * PLANE + (q ^ offset)
                pairs.append((source * tp_count + tp, target * tp_count + z % tp_count))
        landed.append(lax.ppermute(message, ("seq", "tp"), pairs))
    landed, out_weight = lax.optimization_barrier((landed, out_weight))
    own = jnp.stack(landed)
    other = lax.ppermute(own, "tp", [(0, 1), (1, 0)])
    gates = jnp.stack([own, other])

    late = out_weight[:, early:]
    weights_late = [late] + [lax.ppermute(late, "seq", pairs) for pairs in in_plane[1:]]

    def added(first, second):
        return (first.astype(jnp.float32) + second.astype(jnp.float32)).astype(jnp.bfloat16)

    def far_sends(gates, weights):
        (far,) = project(place, gates, weights, (2,), jnp.bfloat16)
        half = far.shape[1] // 2
        return lax.ppermute(far[:, :half], "seq", up), lax.ppermute(far[:, half:], "seq", down)

    def near_sends(gates, weights, far_left, far_right):
        ahead, behind = project(place, gates, weights, (1, planes - 1), jnp.bfloat16)
        half = ahead.shape[1] // 2
        near_right = lax.ppermute(ahead[:, half:], "seq", up)
        near_left = lax.ppermute(behind[:, :half], "seq", down)
        up_sum, down_sum = added(ahead[:, :half], far_left), added(behind[:, half:], far_right)
        return (near_left, near_right), (up_sum, down_sum)

    def sum_sends(sums):
        return lax.ppermute(sums[0], "seq", up), lax.ppermute(sums[1], "seq", down)

    def own_and_near(gates, weights, near):
        (mine,) = project(place, gates, weights, (0,), jnp.float32)
        half = mine.shape[1] // 2
        return mine[:, :half] + near[0].astype(jnp.float32), mine[:, half:] + near[1].astype(jnp.float32)

    weights_early = [weight_early]
    near_early, sums = near_sends(gates, weights_early, *far_sends(gates, weights_early))
    sum_early = sum_sends(sums)
    part_early = own_and_near(gates, weights_early, near_early)
    gates_late, sums, part_early = lax.optimization_barrier((gates, sums, part_early))
    far_late = far_sends(gates_late, weights_late)
    gates_late, sum_early = lax.optimization_barrier((gates_late, sum_early))
    near_late, sums = near_sends(gates_late, weights_late, *far_late)
    sum_late = sum_sends(sums)
    part_late = own_and_near(gates_late, weights_late, near_late)
    columns = [
        part + summed.astype(jnp.float32)
        for part, summed in zip(part_early + part_late, sum_early + sum_late)
    ]
    return jnp.concatenate(columns, axis=1).astype(jnp.bfloat16)


PRECISE = lax.Precision.HIGHEST


def phase_table(period, out_size, in_size, direction):
    out_index = lax.broadcasted_iota(jnp.int32, (out_size, in_size), 0)
    in_index = lax.broadcasted_iota(jnp.int32, (out_size, in_size), 1)
    phase_angle = (out_index * in_index % period).astype(jnp.float32) * (
        direction * 2.0 * math.pi / period
    )
    return (jnp.cos(phase_angle), jnp.sin(phase_angle))


def left_apply(phase, signal):
    return jnp.einsum("kn,cnm->ckm", phase, signal, precision=PRECISE)


def right_apply(signal, phase):
    return jnp.einsum("ckn,nm->ckm", signal, phase, precision=PRECISE)


def forward_spectrum(signal, inner_size):
    channels_here, length = signal.shape
    period = 2 * length
    outer_size = period // inner_size
    blocks = signal.reshape(channels_here, outer_size // 2, inner_size)
    left_re, left_im = phase_table(outer_size, outer_size, outer_size // 2, -1.0)
    section_re = left_apply(left_re, blocks)
    section_im = left_apply(left_im, blocks)
    twist_re, twist_im = phase_table(period, outer_size, inner_size, -1.0)
    turned_re = section_re * twist_re - section_im * twist_im
    turned_im = section_re * twist_im + section_im * twist_re
    right_re, right_im = phase_table(inner_size, inner_size, inner_size, -1.0)
    spec_re = right_apply(turned_re, right_re) - right_apply(turned_im, right_im)
    spec_im = right_apply(turned_re, right_im) + right_apply(turned_im, right_re)
    return (spec_re, spec_im)


def inverse_signal(spec_re, spec_im, length, inner_size):
    channels_here = spec_re.shape[0]
    period = 2 * length
    outer_size = period // inner_size
    right_re, right_im = phase_table(inner_size, inner_size, inner_size, 1.0)
    mid_re = right_apply(spec_re, right_re) - right_apply(spec_im, right_im)
    mid_im = right_apply(spec_re, right_im) + right_apply(spec_im, right_re)
    twist_re, twist_im = phase_table(period, outer_size, inner_size, 1.0)
    turned_re = mid_re * twist_re - mid_im * twist_im
    turned_im = mid_re * twist_im + mid_im * twist_re
    left_re, left_im = phase_table(outer_size, outer_size // 2, outer_size, 1.0)
    signal = left_apply(left_re, turned_re) - left_apply(left_im, turned_im)
    return signal.reshape(channels_here, length) / period


def long_convolve(signal, filters, inner_size):
    length = signal.shape[1]
    data_re, data_im = forward_spectrum(signal, inner_size)
    filt_re, filt_im = forward_spectrum(filters, inner_size)
    prod_re = data_re * filt_re - data_im * filt_im
    prod_im = data_re * filt_im + data_im * filt_re
    return inverse_signal(prod_re, prod_im, length, inner_size)


def by_whole_rows(query_proj, key_proj, value_proj, short_taps, long_filters, out_weight):
    inner_size = query_proj.shape[1] // 2
    streams = (query_proj, key_proj, value_proj)
    query_short, key_short, value_short = filtered_streams(
        streams, last_positions(streams), short_taps
    )
    product = (key_short * value_short).astype(jnp.bfloat16)
    spread = lax.all_to_all(product, "seq", split_axis=0, concat_axis=1, tiled=True)
    mixed_conv = long_convolve(spread.astype(jnp.float32), long_filters, inner_size)
    returned = lax.all_to_all(mixed_conv, "seq", split_axis=1, concat_axis=0, tiled=True)
    gated_out = (query_short * returned).astype(jnp.bfloat16)
    result = lax.dot_general(
        lax.all_gather(gated_out, "tp", axis=0, tiled=True),
        lax.all_gather(out_weight, "seq", axis=0, tiled=True),
        (((0,), (0,)), ((), ())),
        preferred_element_type=jnp.float32,
    )
    return result.astype(jnp.bfloat16)


def solution(mesh):
    planes, cores = mesh.shape["seq"] // PLANE, mesh.shape["tp"]
    plan = by_planes if planes == PLANE and cores == 2 else by_whole_rows
    return jax.shard_map(
        plan,
        mesh=mesh,
        in_specs=(
            P("tp", "seq"),
            P("tp", "seq"),
            P("tp", "seq"),
            P(None, None, "tp"),
            P(("tp", "seq"), None),
            P("seq", "tp"),
        ),
        out_specs=P("seq", "tp"),
        check_vma=False,
    )
```

```python
import functools
import math

import jax
import jax.numpy as jnp
from jax import lax
from jax.experimental import pallas as pl
from jax.experimental.pallas import tpu as pltpu
from jax.sharding import PartitionSpec as P

COLUMN_SHARES = (16, 16)
PLANE = 4
VMEM_LIMIT = 16 * 2**20


def shifted(value, axis, steps):
    count = lax.axis_size(axis)
    initial, last = (max(0, -steps), min(count, count - steps))
    return lax.ppermute(value, axis, [(source, source + steps) for source in range(initial, last)])


def short_filter(extended, tap_weights):
    return (
        tap_weights[0][:, None] * extended[:, 2:]
        + tap_weights[1][:, None] * extended[:, 1:-1]
        + tap_weights[2][:, None] * extended[:, :-2]
    )


def filtered_streams(streams, taps):
    before = shifted(jnp.stack([stream[:, -2:] for stream in streams]), "seq", 1)
    extended = [
        jnp.concatenate([before[index], stream], axis=1).astype(jnp.float32)
        for index, stream in enumerate(streams)
    ]
    return [short_filter(value, tap) for value, tap in zip(extended, taps)]


VMEM = pl.BlockSpec(memory_space=pltpu.VMEM)
SMEM = pl.BlockSpec(memory_space=pltpu.SMEM)
TAIL_ROWS = 16


def tails_kernel(query_ref, key_ref, value_ref, out_ref):
    width = key_ref.shape[1]
    row = lax.broadcasted_iota(jnp.int32, (TAIL_ROWS, width), 0)
    lane = lax.broadcasted_iota(jnp.int32, (TAIL_ROWS, width), 1)
    total = None
    for index, stream in enumerate((query_ref, key_ref, value_ref)):
        picked = (row // 2 == index) & (lane == width - 2 + row % 2)
        term = lax.dot_general(
            jnp.where(picked, 1.0, 0.0).astype(jnp.bfloat16),
            stream[...],
            (((1,), (1,)), ((), ())),
            preferred_element_type=jnp.float32,
        )
        total = term if total is None else total + term
    out_ref[...] = total.astype(out_ref.dtype)


def last_rows(query, key, value):
    return pl.pallas_call(
        tails_kernel,
        out_shape=jax.ShapeDtypeStruct((TAIL_ROWS, key.shape[0]), key.dtype),
        in_specs=[VMEM] * 3,
        out_specs=VMEM,
        compiler_params=pltpu.CompilerParams(vmem_limit_bytes=VMEM_LIMIT),
    )(query, key, value)


def moved_rows(stream):
    width = stream.shape[1]
    row = lax.broadcasted_iota(jnp.int32, (3 * width, width), 0)
    lane = lax.broadcasted_iota(jnp.int32, (3 * width, width), 1)
    picked = jnp.where(lane == row % width - row // width, 1.0, 0.0).astype(stream.dtype)
    moved = lax.dot_general(
        picked, stream, (((1,), (1,)), ((), ())), preferred_element_type=jnp.float32
    )
    return moved[:width], moved[width : 2 * width], moved[2 * width :]


def short_filtered(stream, index, taps_ref, before_ref, spot):
    now, once, twice = moved_rows(stream)
    tap = lambda place: taps_ref[3 * index + place : 3 * index + place + 1, spot]
    second, first = (
        before_ref[:, spot].astype(jnp.float32)[2 * index + place : 2 * index + place + 1]
        for place in range(2)
    )
    row = lax.broadcasted_iota(jnp.int32, now.shape, 0)
    once = jnp.where(row == 0, first, once)
    twice = jnp.where(row == 0, second, jnp.where(row == 1, first, twice))
    return tap(0) * now + tap(1) * once + tap(2) * twice


def product_kernel(taps_ref, before_ref, key_ref, value_ref, out_ref):
    width = key_ref.shape[1]
    for start in range(0, key_ref.shape[0], width):
        spot = pl.ds(start, width)
        key = short_filtered(key_ref[spot], 1, taps_ref, before_ref, spot)
        value = short_filtered(value_ref[spot], 2, taps_ref, before_ref, spot)
        out_ref[spot] = (key * value).T.astype(out_ref.dtype)


def gated_product(taps, before, key, value):
    return pl.pallas_call(
        product_kernel,
        out_shape=jax.ShapeDtypeStruct(key.shape, key.dtype),
        in_specs=[VMEM] * 4,
        out_specs=VMEM,
        compiler_params=pltpu.CompilerParams(vmem_limit_bytes=VMEM_LIMIT),
    )(taps, before, key, value)


def query_kernel(place_ref, taps_ref, before_ref, query_ref, *outs):
    width = query_ref.shape[1]
    for offset, out in enumerate(outs):
        share = jnp.bitwise_xor(place_ref[1], offset)
        for step in range(out.shape[0]):
            spot = pl.ds(pl.multiple_of((share * out.shape[0] + step) * width, width), width)
            query = short_filtered(query_ref[spot], 0, taps_ref, before_ref, spot)
            out[step] = query.astype(out.dtype)


def query_shares(place, taps, before, query, count):
    channels, width = query.shape
    shape = (channels // count // width, width, width)
    return pl.pallas_call(
        query_kernel,
        out_shape=[jax.ShapeDtypeStruct(shape, query.dtype)] * count,
        in_specs=[SMEM] + [VMEM] * 3,
        out_specs=[VMEM] * count,
        compiler_params=pltpu.CompilerParams(vmem_limit_bytes=VMEM_LIMIT),
    )(place, taps, before, query)


BAND = 32
GROUP = 8


def conv_kernel(place_ref, x_ref, h_ref, *rest):
    outs, (signals_f32, turned_filters, shifted_x, result) = rest[:-4], rest[-4:]
    blocks, channels, width = x_ref.shape
    parts = width // BAND
    band_lane = lax.broadcasted_iota(jnp.int32, (BAND, width), 1)
    keep = band_lane > lax.broadcasted_iota(jnp.int32, (BAND, width), 0)
    lane = lax.broadcasted_iota(jnp.int32, (blocks, width), 1)
    row = lax.broadcasted_iota(jnp.int32, (blocks, width), 0)
    square_row = lax.broadcasted_iota(jnp.int32, (width, width), 0)
    square_lane = lax.broadcasted_iota(jnp.int32, (width, width), 1)
    exchange = jnp.where(square_row + square_lane == width - 1, 1.0, 0.0).astype(jnp.bfloat16)
    shifted_x[...] = jnp.zeros(shifted_x.shape, jnp.float32)
    for block in range(blocks):
        signals_f32[block * channels : (block + 1) * channels] = x_ref[block].astype(jnp.float32)
        turned_filters[blocks - 1 - block] = jnp.dot(
            h_ref[:, block * width : (block + 1) * width].astype(jnp.bfloat16),
            exchange,
            preferred_element_type=jnp.float32,
        )

    def one_channel(slot, channel):
        signal = signals_f32[pl.ds(channel, blocks, stride=channels), :]
        shifted_x[slot, 0, blocks : 2 * blocks] = signal
        for part in range(1, parts):
            left = width - BAND * part
            turned = pltpu.roll(signal, left, 1)
            following = jnp.where(row == blocks - 1, 0.0, pltpu.roll(turned, blocks - 1, 0))
            shifted_x[slot, part, blocks : 2 * blocks] = jnp.where(lane < left, turned, following)
            shifted_x[slot, part, blocks - 8 : blocks] = jnp.where(
                (lane[:8] >= left) & (row[:8] == 7), jnp.broadcast_to(turned[:1], (8, width)), 0.0
            )
        earlier = jnp.zeros((BAND, width), jnp.float32)
        bands, signals = [], []
        for lag in range(blocks + 1):
            delayed_filter = jnp.zeros((BAND, width), jnp.float32)
            if lag < blocks:
                delayed_filter = pltpu.roll(
                    jnp.broadcast_to(turned_filters[lag, pl.ds(channel, 1), :], (BAND, width)),
                    1,
                    1,
                    stride=1,
                    stride_axis=0,
                )
            bands.append(jnp.where(keep, delayed_filter, earlier).astype(jnp.bfloat16))
            earlier = delayed_filter
            ahead = [shifted_x[slot, part, lag : lag + blocks, :] for part in range(parts)]
            signals.append(jnp.concatenate(ahead, axis=0).astype(jnp.bfloat16))
        total = lax.dot_general(
            jnp.concatenate(signals, axis=1),
            jnp.concatenate(bands, axis=1),
            (((1,), (1,)), ((), ())),
            preferred_element_type=jnp.float32,
        )
        result[pl.ds(pl.multiple_of(channel * blocks, blocks), blocks), :] = jnp.concatenate(
            [total[part * blocks : (part + 1) * blocks] for part in range(parts)], axis=1
        )

    def one_group(group, carry):
        for slot in range(GROUP):
            one_channel(slot, group * GROUP + slot)
        return carry

    lax.fori_loop(0, channels // GROUP, one_group, 0)
    inner = len(outs)
    for offset, out in enumerate(outs):
        for outer in range(blocks // inner):
            block = outer * inner + jnp.bitwise_xor(place_ref[0], offset)
            out[outer] = result[pl.ds(block, channels, stride=blocks), :].astype(out.dtype)


def convolve(place, product, filters, inner):
    blocks, channels, width = product.shape
    return pl.pallas_call(
        conv_kernel,
        out_shape=[jax.ShapeDtypeStruct((blocks // inner, channels, width), jnp.bfloat16)] * inner,
        in_specs=[SMEM, VMEM, VMEM],
        out_specs=[VMEM] * inner,
        scratch_shapes=[
            pltpu.VMEM((blocks * channels, width), jnp.float32),
            pltpu.VMEM((blocks, channels, width), jnp.float32),
            pltpu.VMEM((GROUP, width // BAND, 2 * blocks + 8, width), jnp.float32),
            pltpu.VMEM((channels * blocks, width), jnp.float32),
        ],
        compiler_params=pltpu.CompilerParams(vmem_limit_bytes=VMEM_LIMIT),
        cost_estimate=pl.CostEstimate(
            flops=16 * channels * width * width * blocks * blocks,
            bytes_accessed=10 * channels * blocks * width,
            transcendentals=0,
        ),
    )(place, product, filters)


def gate_kernel(place_ref, *refs):
    inner = (len(refs) - 1) // 2
    landed, queries, out_ref = refs[:inner], refs[inner:-1], refs[-1]
    share = 2 * (place_ref[1] % 2) + place_ref[2]
    for source, query in enumerate(queries):
        plane = jnp.bitwise_xor(share, source)
        for offset, mixed in enumerate(landed):
            gated = mixed[plane].astype(jnp.float32).T * query[
                jnp.bitwise_xor(place_ref[0], offset)
            ].astype(jnp.float32)
            out_ref[offset, plane] = gated.astype(out_ref.dtype)


def gate(place, landed, queries):
    planes, channels, width = landed[0].shape
    return pl.pallas_call(
        gate_kernel,
        out_shape=jax.ShapeDtypeStruct((len(landed), planes, width, channels), jnp.bfloat16),
        in_specs=[SMEM] + [VMEM] * (len(landed) + len(queries)),
        out_specs=VMEM,
        compiler_params=pltpu.CompilerParams(vmem_limit_bytes=VMEM_LIMIT),
    )(place, *landed, *queries)


def project_kernel(place_ref, own_ref, other_ref, *refs):
    weights, outs = refs[:-4], refs[-4:]
    planes, depth = own_ref.shape[1], own_ref.shape[3]
    inner, outer, core = place_ref[0], place_ref[1], place_ref[2]
    for out, step in zip(outs, STEPS):
        plane = (outer + step) % planes
        total = None
        for index in range(PLANE):
            if len(weights) == 1:
                owner, weight = index, weights[0][2 * depth * index : 2 * depth * (index + 1)]
            elif index + 1 < PLANE:
                owner, weight = jnp.bitwise_xor(inner, index), weights[index][...]
            else:
                owner = jnp.bitwise_xor(inner, index)
                weight = jnp.concatenate([ref[...] for ref in weights[index:]], axis=0)
            mine = jnp.bitwise_xor(owner // 2, core) == 0
            halves = []
            for half in range(2):
                source = jnp.bitwise_xor(2 * (owner % 2) + half, inner)
                halves.append(jnp.where(mine, own_ref[source, plane], other_ref[source, plane]))
            term = jnp.dot(
                jnp.concatenate(halves, axis=1), weight, preferred_element_type=jnp.float32
            )
            total = term if total is None else total + term
        out[...] = total.astype(out.dtype)


STEPS = (2, 1, 3, 0)


def project(place, gates, weights, first, columns):
    _, _, rows, _ = gates[0].shape
    specs = [
        pl.BlockSpec((weight.shape[0], columns), lambda step, place_ref: (0, first // columns))
        for weight in weights
    ]
    whole = pl.BlockSpec(gates[0].shape, lambda step, place_ref: (0,) * 4)
    kinds = [jnp.bfloat16] * 3 + [jnp.float32]
    return pl.pallas_call(
        project_kernel,
        out_shape=[jax.ShapeDtypeStruct((rows, columns), kind) for kind in kinds],
        grid_spec=pltpu.PrefetchScalarGridSpec(
            num_scalar_prefetch=1,
            grid=(1,),
            in_specs=[whole] * 2 + specs,
            out_specs=[pl.BlockSpec((rows, columns), lambda step, place_ref: (0, 0))] * 4,
        ),
        compiler_params=pltpu.CompilerParams(vmem_limit_bytes=VMEM_LIMIT),
        cost_estimate=pl.CostEstimate(flops=rows * columns, bytes_accessed=0, transcendentals=0),
    )(place, *gates, *weights)


def by_planes(query_proj, key_proj, value_proj, short_taps, long_filters, out_weight):
    seq_count, tp_count = lax.axis_size("seq"), lax.axis_size("tp")
    planes = seq_count // PLANE
    place_seq, core = lax.axis_index("seq"), lax.axis_index("tp")
    place = jnp.stack([place_seq % PLANE, place_seq // PLANE, core]).astype(jnp.int32)
    channels, width = long_filters.shape[0], query_proj.shape[1]

    across = [(source, source ^ 1) for source in range(seq_count)]
    along = [(source, source ^ 2) for source in range(seq_count)]
    up = [(source, (source + PLANE) % seq_count) for source in range(seq_count)]
    down = [(target, source) for source, target in up]

    def to_plane_of_rows(message, target_of):
        pairs = []
        for source in range(seq_count):
            z, q = divmod(source, PLANE)
            for tp in range(tp_count):
                share, target_q = target_of(z, q)
                target = (planes // tp_count * tp + share // tp_count) * PLANE + target_q
                pairs.append((source * tp_count + tp, target * tp_count + share % tp_count))
        return lax.ppermute(message, ("seq", "tp"), pairs)

    def from_neighbours(first, count):
        part = out_weight[:, first : first + count]
        return [part, lax.ppermute(part, "seq", across), lax.ppermute(part, "seq", along)]

    def from_corner(part, from_x, from_y):
        half = part.shape[0] // 2
        top = lax.ppermute(from_y[:half], "seq", across)
        end = lax.ppermute(from_x[half:], "seq", along)
        return [part, from_x, from_y, top, end]

    spans, first = [], 0
    for share in COLUMN_SHARES:
        count = out_weight.shape[1] * share // sum(COLUMN_SHARES)
        spans.append((first, count))
        first += count

    groups = [list(range(first, first + PLANE)) for first in range(0, seq_count, PLANE)]
    early = out_weight[:, : spans[0][1]]
    early = lax.all_gather(early, "seq", axis=0, tiled=True, axis_index_groups=groups)
    rows = [[early]]
    taps = jnp.pad(
        short_taps.reshape(-1, short_taps.shape[2]),
        ((0, TAIL_ROWS - short_taps.shape[0] * short_taps.shape[1]), (0, 0)),
    )
    before = shifted(last_rows(query_proj, key_proj, value_proj), "seq", 1)
    product = gated_product(taps, before, key_proj, value_proj)
    product, before = lax.optimization_barrier((product, before))
    spread = lax.all_to_all(
        product.reshape(seq_count, channels, width), "seq", split_axis=0, concat_axis=0, tiled=True
    )
    queries = [
        to_plane_of_rows(message, lambda z, q: (z ^ offset, q))
        for offset, message in enumerate(query_shares(place, taps, before, query_proj, planes))
    ]
    mixed = convolve(place, spread, long_filters, PLANE)
    mixed, queries = lax.optimization_barrier((mixed, queries))
    landed = [
        to_plane_of_rows(message, lambda z, q: (z, q ^ offset))
        for offset, message in enumerate(mixed)
    ]
    landed[0], out_weight = lax.optimization_barrier((landed[0], out_weight))
    rows.append(from_neighbours(*spans[1]))
    own = gate(place, landed, queries)
    gates = [own, lax.ppermute(own, "tp", [(0, 1), (1, 0)])]

    parts, sums, sent = [], [], []
    for index in range(2 * len(spans)):
        if index == 2:
            sent += [lax.ppermute(sums[0], "seq", up), lax.ppermute(sums[1], "seq", down)]
            rows[1], sums = lax.optimization_barrier((rows[1], sums))
            rows[1] = from_corner(*rows[1])
            gates, parts, sums = lax.optimization_barrier((gates, parts, sums))
        elif index == 3:
            gates, sent = lax.optimization_barrier((gates, sent))
        weights, count = rows[index // 2], spans[index // 2][1] // 2
        forth, back = (up, down) if index % 2 == 0 else (down, up)
        far, ahead, behind, mine = project(place, gates, weights, count * (index % 2), count)
        if index % 2 == 1:
            ahead, behind = behind, ahead
        far = lax.ppermute(far, "seq", forth)
        near = lax.ppermute(behind, "seq", back)
        sums.append((ahead.astype(jnp.float32) + far.astype(jnp.float32)).astype(jnp.bfloat16))
        parts.append(mine + near.astype(jnp.float32))
    sent += [lax.ppermute(sums[-2], "seq", up), lax.ppermute(sums[-1], "seq", down)]
    columns = [part + value.astype(jnp.float32) for part, value in zip(parts, sent)]
    return jnp.concatenate(columns, axis=1).astype(jnp.bfloat16)


PRECISE = lax.Precision.HIGHEST


def phase_table(period, out_size, in_size, direction):
    out_index = lax.broadcasted_iota(jnp.int32, (out_size, in_size), 0)
    in_index = lax.broadcasted_iota(jnp.int32, (out_size, in_size), 1)
    phase_angle = (out_index * in_index % period).astype(jnp.float32) * (
        direction * 2.0 * math.pi / period
    )
    return (jnp.cos(phase_angle), jnp.sin(phase_angle))


def left_apply(phase, signal):
    return jnp.einsum("kn,cnm->ckm", phase, signal, precision=PRECISE)


def right_apply(signal, phase):
    return jnp.einsum("ckn,nm->ckm", signal, phase, precision=PRECISE)


def forward_spectrum(signal, inner_size):
    channels_here, length = signal.shape
    period = 2 * length
    outer_size = period // inner_size
    blocks = signal.reshape(channels_here, outer_size // 2, inner_size)
    left_re, left_im = phase_table(outer_size, outer_size, outer_size // 2, -1.0)
    section_re = left_apply(left_re, blocks)
    section_im = left_apply(left_im, blocks)
    twist_re, twist_im = phase_table(period, outer_size, inner_size, -1.0)
    turned_re = section_re * twist_re - section_im * twist_im
    turned_im = section_re * twist_im + section_im * twist_re
    right_re, right_im = phase_table(inner_size, inner_size, inner_size, -1.0)
    spec_re = right_apply(turned_re, right_re) - right_apply(turned_im, right_im)
    spec_im = right_apply(turned_re, right_im) + right_apply(turned_im, right_re)
    return (spec_re, spec_im)


def inverse_signal(spec_re, spec_im, length, inner_size):
    channels_here = spec_re.shape[0]
    period = 2 * length
    outer_size = period // inner_size
    right_re, right_im = phase_table(inner_size, inner_size, inner_size, 1.0)
    mid_re = right_apply(spec_re, right_re) - right_apply(spec_im, right_im)
    mid_im = right_apply(spec_re, right_im) + right_apply(spec_im, right_re)
    twist_re, twist_im = phase_table(period, outer_size, inner_size, 1.0)
    turned_re = mid_re * twist_re - mid_im * twist_im
    turned_im = mid_re * twist_im + mid_im * twist_re
    left_re, left_im = phase_table(outer_size, outer_size // 2, outer_size, 1.0)
    signal = left_apply(left_re, turned_re) - left_apply(left_im, turned_im)
    return signal.reshape(channels_here, length) / period


def long_convolve(signal, filters, inner_size):
    length = signal.shape[1]
    data_re, data_im = forward_spectrum(signal, inner_size)
    filt_re, filt_im = forward_spectrum(filters, inner_size)
    prod_re = data_re * filt_re - data_im * filt_im
    prod_im = data_re * filt_im + data_im * filt_re
    return inverse_signal(prod_re, prod_im, length, inner_size)


def by_whole_rows(query_proj, key_proj, value_proj, short_taps, long_filters, out_weight):
    inner_size = query_proj.shape[1] // 2
    query_short, key_short, value_short = filtered_streams(
        (query_proj, key_proj, value_proj), short_taps
    )
    product = (key_short * value_short).astype(jnp.bfloat16)
    spread = lax.all_to_all(product, "seq", split_axis=0, concat_axis=1, tiled=True)
    mixed_conv = long_convolve(spread.astype(jnp.float32), long_filters, inner_size)
    returned = lax.all_to_all(mixed_conv, "seq", split_axis=1, concat_axis=0, tiled=True)
    gated_out = (query_short * returned).astype(jnp.bfloat16)
    result = lax.dot_general(
        lax.all_gather(gated_out, "tp", axis=0, tiled=True),
        lax.all_gather(out_weight, "seq", axis=0, tiled=True),
        (((0,), (0,)), ((), ())),
        preferred_element_type=jnp.float32,
    )
    return result.astype(jnp.bfloat16)


def solution(mesh):
    planes, cores = mesh.shape["seq"] // PLANE, mesh.shape["tp"]
    plan = by_planes if planes == PLANE and cores == 2 else by_whole_rows
    return jax.shard_map(
        plan,
        mesh=mesh,
        in_specs=(
            P("tp", "seq"),
            P("tp", "seq"),
            P("tp", "seq"),
            P(None, None, "tp"),
            P(("tp", "seq"), None),
            P("seq", "tp"),
        ),
        out_specs=P("seq", "tp"),
        check_vma=False,
    )
```

```python
import functools
import math

import jax
import jax.numpy as jnp
from jax import lax
from jax.experimental import pallas as pl
from jax.experimental.pallas import tpu as pltpu
from jax.sharding import PartitionSpec as P

COLUMN_SHARES = (14, 18)
PLANE = 4
VMEM_LIMIT = 16 * 2**20


def shifted(value, axis, steps):
    count = lax.axis_size(axis)
    initial, last = (max(0, -steps), min(count, count - steps))
    return lax.ppermute(value, axis, [(source, source + steps) for source in range(initial, last)])


def short_filter(extended, tap_weights):
    return (
        tap_weights[0][:, None] * extended[:, 2:]
        + tap_weights[1][:, None] * extended[:, 1:-1]
        + tap_weights[2][:, None] * extended[:, :-2]
    )


def filtered_streams(streams, taps):
    before = shifted(jnp.stack([stream[:, -2:] for stream in streams]), "seq", 1)
    extended = [
        jnp.concatenate([before[index], stream], axis=1).astype(jnp.float32)
        for index, stream in enumerate(streams)
    ]
    return [short_filter(value, tap) for value, tap in zip(extended, taps)]


VMEM = pl.BlockSpec(memory_space=pltpu.VMEM)
SMEM = pl.BlockSpec(memory_space=pltpu.SMEM)
EDGE_ROWS = 16


def picked_rows(stream, pairs):
    width = stream.shape[1]
    row = lax.broadcasted_iota(jnp.int32, (EDGE_ROWS, width), 0)
    lane = lax.broadcasted_iota(jnp.int32, (EDGE_ROWS, width), 1)
    picked = functools.reduce(
        jnp.logical_or, [(row == out) & (lane == position) for out, position in pairs]
    )
    return lax.dot_general(
        jnp.where(picked, 1.0, 0.0).astype(stream.dtype),
        stream,
        (((1,), (1,)), ((), ())),
        preferred_element_type=jnp.float32,
    )


def moved_rows(stream):
    width = stream.shape[1]
    row = lax.broadcasted_iota(jnp.int32, (3 * width, width), 0)
    lane = lax.broadcasted_iota(jnp.int32, (3 * width, width), 1)
    picked = jnp.where(lane == row % width - row // width, 1.0, 0.0).astype(stream.dtype)
    moved = lax.dot_general(
        picked, stream, (((1,), (1,)), ((), ())), preferred_element_type=jnp.float32
    )
    return moved[:width], moved[width : 2 * width], moved[2 * width :]


def short_filtered(stream, index, taps_ref, spot):
    now, once, twice = moved_rows(stream)
    tap = lambda place: taps_ref[3 * index + place : 3 * index + place + 1, spot]
    return tap(0) * now + tap(1) * once + tap(2) * twice


def product_kernel(taps_ref, key_ref, value_ref, out_ref):
    blocks, rows, width = out_ref.shape
    for block in range(blocks):
        spot = pl.ds(block * width, width)
        key, value = key_ref[spot], value_ref[spot]
        product = short_filtered(key, 1, taps_ref, spot)
        product = product * short_filtered(value, 2, taps_ref, spot)
        out_ref[block, :width] = product.T.astype(out_ref.dtype)
        places = (0, 1, width - 2, width - 1)
        edges = picked_rows(key, list(enumerate(places)))
        edges = edges + picked_rows(value, [(4 + out, place) for out, place in enumerate(places)])
        out_ref[block, width:] = edges.astype(out_ref.dtype)


def gated_product(taps, key, value):
    channels, width = key.shape
    return pl.pallas_call(
        product_kernel,
        out_shape=jax.ShapeDtypeStruct((channels // width, width + EDGE_ROWS, width), key.dtype),
        in_specs=[VMEM] * 3,
        out_specs=VMEM,
        compiler_params=pltpu.CompilerParams(vmem_limit_bytes=VMEM_LIMIT),
    )(taps, key, value)


def first_products(taps, edges, earlier):
    short = []
    for stream in range(2):
        tap = [taps[3 * (stream + 1) + place : 3 * (stream + 1) + place + 1] for place in range(3)]
        start, then = (edges[4 * stream + place : 4 * stream + place + 1] for place in range(2))
        second, first = (earlier[4 * stream + place : 4 * stream + place + 1] for place in (2, 3))
        short.append(
            (
                tap[0] * start + tap[1] * first + tap[2] * second,
                tap[0] * then + tap[1] * start + tap[2] * first,
            )
        )
    return [(key * value).astype(jnp.bfloat16).astype(jnp.float32) for key, value in zip(*short)]


BAND = 32
GROUP = 16


def conv_kernel(taps_ref, x_ref, h_ref, result, signals_f32, turned_filters, shifted_x):
    blocks, width = x_ref.shape[0], x_ref.shape[2]
    channels = h_ref.shape[0]
    parts = width // BAND
    band_lane = lax.broadcasted_iota(jnp.int32, (BAND, width), 1)
    keep = band_lane > lax.broadcasted_iota(jnp.int32, (BAND, width), 0)
    lane = lax.broadcasted_iota(jnp.int32, (blocks, width), 1)
    row = lax.broadcasted_iota(jnp.int32, (blocks, width), 0)
    square_row = lax.broadcasted_iota(jnp.int32, (width, width), 0)
    square_lane = lax.broadcasted_iota(jnp.int32, (width, width), 1)
    exchange = jnp.where(square_row + square_lane == width - 1, 1.0, 0.0).astype(jnp.bfloat16)
    shifted_x[...] = jnp.zeros(shifted_x.shape, jnp.float32)
    tile_lane = lax.broadcasted_iota(jnp.int32, (channels, width), 1)
    taps = taps_ref[...]
    earlier_edges = jnp.zeros((EDGE_ROWS, channels), jnp.float32)
    for block in range(blocks):
        edges = x_ref[block, channels:].astype(jnp.float32)
        pair = first_products(taps, edges, earlier_edges)
        earlier_edges = edges
        pair_row = lax.broadcasted_iota(jnp.int32, (8, channels), 0)
        pair = jnp.where(pair_row == 0, pair[0], jnp.where(pair_row == 1, pair[1], 0.0)).T
        tile = x_ref[block, :channels].astype(jnp.float32)
        tile = jnp.where(tile_lane == 0, pair[:, :1], jnp.where(tile_lane == 1, pair[:, 1:2], tile))
        signals_f32[block * channels : (block + 1) * channels] = tile
        turned_filters[blocks - 1 - block] = jnp.dot(
            h_ref[:, block * width : (block + 1) * width].astype(jnp.bfloat16),
            exchange,
            preferred_element_type=jnp.float32,
        )

    def one_channel(slot, channel):
        signal = signals_f32[pl.ds(channel, blocks, stride=channels), :]
        shifted_x[slot, 0, blocks : 2 * blocks] = signal
        for part in range(1, parts):
            left = width - BAND * part
            turned = pltpu.roll(signal, left, 1)
            following = jnp.where(row == blocks - 1, 0.0, pltpu.roll(turned, blocks - 1, 0))
            shifted_x[slot, part, blocks : 2 * blocks] = jnp.where(lane < left, turned, following)
            shifted_x[slot, part, blocks - 8 : blocks] = jnp.where(
                (lane[:8] >= left) & (row[:8] == 7), jnp.broadcast_to(turned[:1], (8, width)), 0.0
            )
        earlier = jnp.zeros((BAND, width), jnp.float32)
        bands, signals = [], []
        for lag in range(blocks + 1):
            delayed_filter = jnp.zeros((BAND, width), jnp.float32)
            if lag < blocks:
                delayed_filter = pltpu.roll(
                    jnp.broadcast_to(turned_filters[lag, pl.ds(channel, 1), :], (BAND, width)),
                    1,
                    1,
                    stride=1,
                    stride_axis=0,
                )
            bands.append(jnp.where(keep, delayed_filter, earlier).astype(jnp.bfloat16))
            earlier = delayed_filter
            ahead = [shifted_x[slot, part, lag : lag + blocks, :] for part in range(parts)]
            signals.append(jnp.concatenate(ahead, axis=0).astype(jnp.bfloat16))
        total = lax.dot_general(
            jnp.concatenate(signals, axis=1),
            jnp.concatenate(bands, axis=1),
            (((1,), (1,)), ((), ())),
            preferred_element_type=jnp.float32,
        )
        result[pl.ds(pl.multiple_of(channel * blocks, blocks), blocks), :] = jnp.concatenate(
            [total[part * blocks : (part + 1) * blocks] for part in range(parts)], axis=1
        )

    def one_group(group, carry):
        for slot in range(GROUP):
            one_channel(slot, group * GROUP + slot)
        return carry

    lax.fori_loop(0, channels // GROUP, one_group, 0)


def convolve(taps, product, filters):
    blocks, _, width = product.shape
    channels = filters.shape[0]
    return pl.pallas_call(
        conv_kernel,
        out_shape=jax.ShapeDtypeStruct((channels * blocks, width), jnp.float32),
        in_specs=[VMEM] * 3,
        out_specs=VMEM,
        scratch_shapes=[
            pltpu.VMEM((blocks * channels, width), jnp.float32),
            pltpu.VMEM((blocks, channels, width), jnp.float32),
            pltpu.VMEM((GROUP, width // BAND, 2 * blocks + 8, width), jnp.float32),
        ],
        compiler_params=pltpu.CompilerParams(vmem_limit_bytes=VMEM_LIMIT),
        cost_estimate=pl.CostEstimate(
            flops=16 * channels * width * width * blocks * blocks,
            bytes_accessed=10 * channels * blocks * width,
            transcendentals=0,
        ),
    )(taps, product, filters)


def gate_kernel(place_ref, taps_ref, q_ref, y_ref, *outs):
    blocks, channels, width = q_ref.shape
    lane = lax.broadcasted_iota(jnp.int32, (channels, width), 1)
    columns = taps_ref[...].T
    taps = [jnp.broadcast_to(columns[:, place : place + 1], lane.shape) for place in range(3)]
    inner = len(outs)
    for offset, out in enumerate(outs):
        for outer in range(blocks // inner):
            block = outer * inner + jnp.bitwise_xor(place_ref[0], offset)
            query = q_ref[block].astype(jnp.float32)
            earlier = q_ref[jnp.maximum(block - 1, 0)].astype(jnp.float32)
            earlier = jnp.where(block > 0, earlier, 0.0)
            once, twice = (
                jnp.where(lane >= steps, pltpu.roll(query, steps, 1), pltpu.roll(earlier, steps, 1))
                for steps in (1, 2)
            )
            query_short = taps[0] * query + taps[1] * once + taps[2] * twice
            gated = query_short * y_ref[pl.ds(block, channels, stride=blocks), :]
            out[outer] = gated.T.astype(out.dtype)


def gate(place, taps, query, mixed, inner):
    blocks, channels, width = query.shape
    return pl.pallas_call(
        gate_kernel,
        out_shape=[jax.ShapeDtypeStruct((blocks // inner, width, channels), jnp.bfloat16)] * inner,
        in_specs=[SMEM] + [VMEM] * 3,
        out_specs=[VMEM] * inner,
        compiler_params=pltpu.CompilerParams(vmem_limit_bytes=VMEM_LIMIT),
    )(place, taps, query, mixed)


def project_kernel(place_ref, own_ref, other_ref, *refs):
    weights, outs = refs[:-4], refs[-4:]
    planes, depth = own_ref.shape[1], own_ref.shape[3]
    inner, outer, core = place_ref[0], place_ref[1], place_ref[2]
    for out, step in zip(outs, STEPS):
        plane = (outer + step) % planes
        total = None
        for index in range(PLANE):
            if len(weights) == 1:
                owner, weight = index, weights[0][2 * depth * index : 2 * depth * (index + 1)]
            elif index + 1 < PLANE:
                owner, weight = jnp.bitwise_xor(inner, index), weights[index][...]
            else:
                owner = jnp.bitwise_xor(inner, index)
                weight = jnp.concatenate([ref[...] for ref in weights[index:]], axis=0)
            mine = jnp.bitwise_xor(owner // 2, core) == 0
            halves = []
            for half in range(2):
                source = jnp.bitwise_xor(2 * (owner % 2) + half, inner)
                halves.append(jnp.where(mine, own_ref[source, plane], other_ref[source, plane]))
            term = jnp.dot(
                jnp.concatenate(halves, axis=1), weight, preferred_element_type=jnp.float32
            )
            total = term if total is None else total + term
        out[...] = total.astype(out.dtype)


STEPS = (2, 1, 3, 0)


def project(place, gates, weights, columns):
    _, _, rows, _ = gates[0].shape
    specs = [
        pl.BlockSpec(
            (weight.shape[0], columns),
            functools.partial(lambda block, step, place_ref: (0, block), first // columns),
        )
        for weight, first in weights
    ]
    whole = pl.BlockSpec(gates[0].shape, lambda step, place_ref: (0,) * 4)
    kinds = [jnp.bfloat16] * 3 + [jnp.float32]
    return pl.pallas_call(
        project_kernel,
        out_shape=[jax.ShapeDtypeStruct((rows, columns), kind) for kind in kinds],
        grid_spec=pltpu.PrefetchScalarGridSpec(
            num_scalar_prefetch=1,
            grid=(1,),
            in_specs=[whole] * 2 + specs,
            out_specs=[pl.BlockSpec((rows, columns), lambda step, place_ref: (0, 0))] * 4,
        ),
        compiler_params=pltpu.CompilerParams(vmem_limit_bytes=VMEM_LIMIT),
        cost_estimate=pl.CostEstimate(flops=rows * columns, bytes_accessed=0, transcendentals=0),
    )(place, *gates, *[weight for weight, _ in weights])


def by_planes(query_proj, key_proj, value_proj, short_taps, long_filters, out_weight):
    seq_count, tp_count = lax.axis_size("seq"), lax.axis_size("tp")
    planes = seq_count // PLANE
    place_seq, core = lax.axis_index("seq"), lax.axis_index("tp")
    place = jnp.stack([place_seq % PLANE, place_seq // PLANE, core]).astype(jnp.int32)
    channels, width = long_filters.shape[0], query_proj.shape[1]

    across = [(source, source ^ 1) for source in range(seq_count)]
    along = [(source, source ^ 2) for source in range(seq_count)]
    up = [(source, (source + PLANE) % seq_count) for source in range(seq_count)]
    down = [(target, source) for source, target in up]

    def to_plane_of_rows(message, offset):
        pairs = []
        for source in range(seq_count):
            z, q = divmod(source, PLANE)
            for tp in range(tp_count):
                target = (planes // tp_count * tp + z // tp_count) * PLANE + (q ^ offset)
                pairs.append((source * tp_count + tp, target * tp_count + z % tp_count))
        return lax.ppermute(message, ("seq", "tp"), pairs)

    def from_neighbours(first, count):
        part = out_weight[:, first : first + count]
        return [part, lax.ppermute(part, "seq", across), lax.ppermute(part, "seq", along)]

    def from_corner(part, from_x, from_y, first, count):
        half = part.shape[0] // 2
        top = lax.ppermute(from_y[:half, first : first + count], "seq", across)
        end = lax.ppermute(from_x[half:, first : first + count], "seq", along)
        return [(part, first), (from_x, first), (from_y, first), (top, 0), (end, 0)]

    spans, first = [], 0
    for share in COLUMN_SHARES:
        count = out_weight.shape[1] * share // sum(COLUMN_SHARES)
        spans.append((first, count))
        first += count

    groups = [list(range(first, first + PLANE)) for first in range(0, seq_count, PLANE)]
    early = out_weight[:, : spans[0][1]]
    early = lax.all_gather(early, "seq", axis=0, tiled=True, axis_index_groups=groups)
    half = spans[0][1] // 2
    halves = [([(early, 0)], half), ([(early, half)], half)]
    taps = jnp.pad(
        short_taps.reshape(-1, short_taps.shape[2]),
        ((0, EDGE_ROWS - short_taps.shape[0] * short_taps.shape[1]), (0, 0)),
    )
    product = gated_product(taps, key_proj, value_proj)
    spread = lax.all_to_all(product, "seq", split_axis=0, concat_axis=0, tiled=True)
    taps_here = lax.dynamic_slice_in_dim(taps, place_seq * channels, channels, axis=1)
    spread, query_proj = lax.optimization_barrier((spread, query_proj))
    query = lax.all_to_all(
        query_proj.reshape(seq_count, channels, width), "seq", split_axis=0, concat_axis=0, tiled=True
    )
    mixed = convolve(taps_here, spread, long_filters)
    landed = [
        to_plane_of_rows(message, offset)
        for offset, message in enumerate(gate(place, taps_here, query, mixed, PLANE))
    ]
    landed[0], out_weight = lax.optimization_barrier((landed[0], out_weight))
    late = from_neighbours(*spans[1])
    own = jnp.stack(landed)
    gates = [own, lax.ppermute(own, "tp", [(0, 1), (1, 0)])]

    parts, sums, sent = [], [], []
    for index in range(4):
        if index == 2:
            sent += [lax.ppermute(sums[0], "seq", up), lax.ppermute(sums[1], "seq", down)]
            late, sums = lax.optimization_barrier((late, sums))
            half = spans[1][1] // 2
            halves += [(from_corner(*late, first, half), half) for first in (0, half)]
            gates, parts, sums = lax.optimization_barrier((gates, parts, sums))
        elif index == 3:
            gates, sent = lax.optimization_barrier((gates, sent))
        weights, count = halves[index]
        forth, back = (up, down) if index % 2 == 0 else (down, up)
        far, ahead, behind, mine = project(place, gates, weights, count)
        if index % 2 == 1:
            ahead, behind = behind, ahead
        far = lax.ppermute(far, "seq", forth)
        near = lax.ppermute(behind, "seq", back)
        sums.append((ahead.astype(jnp.float32) + far.astype(jnp.float32)).astype(jnp.bfloat16))
        parts.append(mine + near.astype(jnp.float32))
    sent += [lax.ppermute(sums[-2], "seq", up), lax.ppermute(sums[-1], "seq", down)]
    columns = [part + value.astype(jnp.float32) for part, value in zip(parts, sent)]
    return jnp.concatenate(columns, axis=1).astype(jnp.bfloat16)


PRECISE = lax.Precision.HIGHEST


def phase_table(period, out_size, in_size, direction):
    out_index = lax.broadcasted_iota(jnp.int32, (out_size, in_size), 0)
    in_index = lax.broadcasted_iota(jnp.int32, (out_size, in_size), 1)
    phase_angle = (out_index * in_index % period).astype(jnp.float32) * (
        direction * 2.0 * math.pi / period
    )
    return (jnp.cos(phase_angle), jnp.sin(phase_angle))


def left_apply(phase, signal):
    return jnp.einsum("kn,cnm->ckm", phase, signal, precision=PRECISE)


def right_apply(signal, phase):
    return jnp.einsum("ckn,nm->ckm", signal, phase, precision=PRECISE)


def forward_spectrum(signal, inner_size):
    channels_here, length = signal.shape
    period = 2 * length
    outer_size = period // inner_size
    blocks = signal.reshape(channels_here, outer_size // 2, inner_size)
    left_re, left_im = phase_table(outer_size, outer_size, outer_size // 2, -1.0)
    section_re = left_apply(left_re, blocks)
    section_im = left_apply(left_im, blocks)
    twist_re, twist_im = phase_table(period, outer_size, inner_size, -1.0)
    turned_re = section_re * twist_re - section_im * twist_im
    turned_im = section_re * twist_im + section_im * twist_re
    right_re, right_im = phase_table(inner_size, inner_size, inner_size, -1.0)
    spec_re = right_apply(turned_re, right_re) - right_apply(turned_im, right_im)
    spec_im = right_apply(turned_re, right_im) + right_apply(turned_im, right_re)
    return (spec_re, spec_im)


def inverse_signal(spec_re, spec_im, length, inner_size):
    channels_here = spec_re.shape[0]
    period = 2 * length
    outer_size = period // inner_size
    right_re, right_im = phase_table(inner_size, inner_size, inner_size, 1.0)
    mid_re = right_apply(spec_re, right_re) - right_apply(spec_im, right_im)
    mid_im = right_apply(spec_re, right_im) + right_apply(spec_im, right_re)
    twist_re, twist_im = phase_table(period, outer_size, inner_size, 1.0)
    turned_re = mid_re * twist_re - mid_im * twist_im
    turned_im = mid_re * twist_im + mid_im * twist_re
    left_re, left_im = phase_table(outer_size, outer_size // 2, outer_size, 1.0)
    signal = left_apply(left_re, turned_re) - left_apply(left_im, turned_im)
    return signal.reshape(channels_here, length) / period


def long_convolve(signal, filters, inner_size):
    length = signal.shape[1]
    data_re, data_im = forward_spectrum(signal, inner_size)
    filt_re, filt_im = forward_spectrum(filters, inner_size)
    prod_re = data_re * filt_re - data_im * filt_im
    prod_im = data_re * filt_im + data_im * filt_re
    return inverse_signal(prod_re, prod_im, length, inner_size)


def by_whole_rows(query_proj, key_proj, value_proj, short_taps, long_filters, out_weight):
    inner_size = query_proj.shape[1] // 2
    query_short, key_short, value_short = filtered_streams(
        (query_proj, key_proj, value_proj), short_taps
    )
    product = (key_short * value_short).astype(jnp.bfloat16)
    spread = lax.all_to_all(product, "seq", split_axis=0, concat_axis=1, tiled=True)
    mixed_conv = long_convolve(spread.astype(jnp.float32), long_filters, inner_size)
    returned = lax.all_to_all(mixed_conv, "seq", split_axis=1, concat_axis=0, tiled=True)
    gated_out = (query_short * returned).astype(jnp.bfloat16)
    result = lax.dot_general(
        lax.all_gather(gated_out, "tp", axis=0, tiled=True),
        lax.all_gather(out_weight, "seq", axis=0, tiled=True),
        (((0,), (0,)), ((), ())),
        preferred_element_type=jnp.float32,
    )
    return result.astype(jnp.bfloat16)


def solution(mesh):
    planes, cores = mesh.shape["seq"] // PLANE, mesh.shape["tp"]
    plan = by_planes if planes == PLANE and cores == 2 else by_whole_rows
    return jax.shard_map(
        plan,
        mesh=mesh,
        in_specs=(
            P("tp", "seq"),
            P("tp", "seq"),
            P("tp", "seq"),
            P(None, None, "tp"),
            P(("tp", "seq"), None),
            P("seq", "tp"),
        ),
        out_specs=P("seq", "tp"),
        check_vma=False,
    )
```

```python
import functools
import math

import jax
import jax.numpy as jnp
from jax import lax
from jax.experimental import pallas as pl
from jax.experimental.pallas import tpu as pltpu
from jax.sharding import PartitionSpec as P

COLUMN_SHARES = (14, 18)
PLANE = 4
VMEM_LIMIT = 16 * 2**20


def shifted(value, axis, steps):
    count = lax.axis_size(axis)
    initial, last = (max(0, -steps), min(count, count - steps))
    return lax.ppermute(value, axis, [(source, source + steps) for source in range(initial, last)])


def short_filter(extended, tap_weights):
    return (
        tap_weights[0][:, None] * extended[:, 2:]
        + tap_weights[1][:, None] * extended[:, 1:-1]
        + tap_weights[2][:, None] * extended[:, :-2]
    )


def filtered_streams(streams, taps):
    before = shifted(jnp.stack([stream[:, -2:] for stream in streams]), "seq", 1)
    extended = [
        jnp.concatenate([before[index], stream], axis=1).astype(jnp.float32)
        for index, stream in enumerate(streams)
    ]
    return [short_filter(value, tap) for value, tap in zip(extended, taps)]


VMEM = pl.BlockSpec(memory_space=pltpu.VMEM)
SMEM = pl.BlockSpec(memory_space=pltpu.SMEM)
EDGE_ROWS = 16


def picked_rows(stream, pairs):
    width = stream.shape[1]
    row = lax.broadcasted_iota(jnp.int32, (EDGE_ROWS, width), 0)
    lane = lax.broadcasted_iota(jnp.int32, (EDGE_ROWS, width), 1)
    picked = functools.reduce(
        jnp.logical_or, [(row == out) & (lane == position) for out, position in pairs]
    )
    return lax.dot_general(
        jnp.where(picked, 1.0, 0.0).astype(stream.dtype),
        stream,
        (((1,), (1,)), ((), ())),
        preferred_element_type=jnp.float32,
    )


def moved_rows(stream):
    width = stream.shape[1]
    row = lax.broadcasted_iota(jnp.int32, (3 * width, width), 0)
    lane = lax.broadcasted_iota(jnp.int32, (3 * width, width), 1)
    picked = jnp.where(lane == row % width - row // width, 1.0, 0.0).astype(stream.dtype)
    moved = lax.dot_general(
        picked, stream, (((1,), (1,)), ((), ())), preferred_element_type=jnp.float32
    )
    return moved[:width], moved[width : 2 * width], moved[2 * width :]


def short_filtered(stream, index, taps_ref, spot):
    now, once, twice = moved_rows(stream)
    tap = lambda place: taps_ref[3 * index + place : 3 * index + place + 1, spot]
    return tap(0) * now + tap(1) * once + tap(2) * twice


def product_kernel(taps_ref, key_ref, value_ref, out_ref):
    blocks, rows, width = out_ref.shape
    for block in range(blocks):
        spot = pl.ds(block * width, width)
        key, value = key_ref[spot], value_ref[spot]
        product = short_filtered(key, 1, taps_ref, spot)
        product = product * short_filtered(value, 2, taps_ref, spot)
        out_ref[block, :width] = product.T.astype(out_ref.dtype)
        places = (0, 1, width - 2, width - 1)
        edges = picked_rows(key, list(enumerate(places)))
        edges = edges + picked_rows(value, [(4 + out, place) for out, place in enumerate(places)])
        out_ref[block, width:] = edges.astype(out_ref.dtype)


def gated_product(taps, key, value):
    channels, width = key.shape
    return pl.pallas_call(
        product_kernel,
        out_shape=jax.ShapeDtypeStruct((channels // width, width + EDGE_ROWS, width), key.dtype),
        in_specs=[VMEM] * 3,
        out_specs=VMEM,
        compiler_params=pltpu.CompilerParams(vmem_limit_bytes=VMEM_LIMIT),
    )(taps, key, value)


def first_products(taps, edges, earlier):
    short = []
    for stream in range(2):
        tap = [taps[3 * (stream + 1) + place : 3 * (stream + 1) + place + 1] for place in range(3)]
        start, then = (edges[4 * stream + place : 4 * stream + place + 1] for place in range(2))
        second, first = (earlier[4 * stream + place : 4 * stream + place + 1] for place in (2, 3))
        short.append(
            (
                tap[0] * start + tap[1] * first + tap[2] * second,
                tap[0] * then + tap[1] * start + tap[2] * first,
            )
        )
    return [(key * value).astype(jnp.bfloat16).astype(jnp.float32) for key, value in zip(*short)]


BAND = 64
GROUP = 16


def conv_kernel(taps_ref, x_ref, h_ref, result, signals_f32, turned_filters, shifted_x):
    blocks, width = x_ref.shape[0], x_ref.shape[2]
    channels = h_ref.shape[0]
    parts = width // BAND
    band_lane = lax.broadcasted_iota(jnp.int32, (BAND, width), 1)
    keep = band_lane > lax.broadcasted_iota(jnp.int32, (BAND, width), 0)
    lane = lax.broadcasted_iota(jnp.int32, (blocks, width), 1)
    row = lax.broadcasted_iota(jnp.int32, (blocks, width), 0)
    square_row = lax.broadcasted_iota(jnp.int32, (width, width), 0)
    square_lane = lax.broadcasted_iota(jnp.int32, (width, width), 1)
    exchange = jnp.where(square_row + square_lane == width - 1, 1.0, 0.0).astype(jnp.bfloat16)
    shifted_x[...] = jnp.zeros(shifted_x.shape, jnp.float32)
    tile_lane = lax.broadcasted_iota(jnp.int32, (channels, width), 1)
    taps = taps_ref[...]
    earlier_edges = jnp.zeros((EDGE_ROWS, channels), jnp.float32)
    for block in range(blocks):
        edges = x_ref[block, channels:].astype(jnp.float32)
        pair = first_products(taps, edges, earlier_edges)
        earlier_edges = edges
        pair_row = lax.broadcasted_iota(jnp.int32, (8, channels), 0)
        pair = jnp.where(pair_row == 0, pair[0], jnp.where(pair_row == 1, pair[1], 0.0)).T
        tile = x_ref[block, :channels].astype(jnp.float32)
        tile = jnp.where(tile_lane == 0, pair[:, :1], jnp.where(tile_lane == 1, pair[:, 1:2], tile))
        signals_f32[block * channels : (block + 1) * channels] = tile
        turned_filters[blocks - 1 - block] = jnp.dot(
            h_ref[:, block * width : (block + 1) * width].astype(jnp.bfloat16),
            exchange,
            preferred_element_type=jnp.float32,
        )

    def one_channel(slot, channel):
        signal = signals_f32[pl.ds(channel, blocks, stride=channels), :]
        shifted_x[slot, 0, blocks : 2 * blocks] = signal
        for part in range(1, parts):
            left = width - BAND * part
            turned = pltpu.roll(signal, left, 1)
            following = jnp.where(row == blocks - 1, 0.0, pltpu.roll(turned, blocks - 1, 0))
            shifted_x[slot, part, blocks : 2 * blocks] = jnp.where(lane < left, turned, following)
            shifted_x[slot, part, blocks - 8 : blocks] = jnp.where(
                (lane[:8] >= left) & (row[:8] == 7), jnp.broadcast_to(turned[:1], (8, width)), 0.0
            )
        earlier = jnp.zeros((BAND, width), jnp.float32)
        bands, signals = [], []
        for lag in range(blocks + 1):
            delayed_filter = jnp.zeros((BAND, width), jnp.float32)
            if lag < blocks:
                delayed_filter = pltpu.roll(
                    jnp.broadcast_to(turned_filters[lag, pl.ds(channel, 1), :], (BAND, width)),
                    1,
                    1,
                    stride=1,
                    stride_axis=0,
                )
            bands.append(jnp.where(keep, delayed_filter, earlier).astype(jnp.bfloat16))
            earlier = delayed_filter
            ahead = [shifted_x[slot, part, lag : lag + blocks, :] for part in range(parts)]
            signals.append(jnp.concatenate(ahead, axis=0).astype(jnp.bfloat16))
        total = lax.dot_general(
            jnp.concatenate(signals, axis=1),
            jnp.concatenate(bands, axis=1),
            (((1,), (1,)), ((), ())),
            preferred_element_type=jnp.float32,
        )
        result[pl.ds(pl.multiple_of(channel * blocks, blocks), blocks), :] = jnp.concatenate(
            [total[part * blocks : (part + 1) * blocks] for part in range(parts)], axis=1
        )

    def one_group(group, carry):
        for slot in range(GROUP):
            one_channel(slot, group * GROUP + slot)
        return carry

    lax.fori_loop(0, channels // GROUP, one_group, 0)


def convolve(taps, product, filters):
    blocks, _, width = product.shape
    channels = filters.shape[0]
    return pl.pallas_call(
        conv_kernel,
        out_shape=jax.ShapeDtypeStruct((channels * blocks, width), jnp.float32),
        in_specs=[VMEM] * 3,
        out_specs=VMEM,
        scratch_shapes=[
            pltpu.VMEM((blocks * channels, width), jnp.float32),
            pltpu.VMEM((blocks, channels, width), jnp.float32),
            pltpu.VMEM((GROUP, width // BAND, 2 * blocks + 8, width), jnp.float32),
        ],
        compiler_params=pltpu.CompilerParams(vmem_limit_bytes=VMEM_LIMIT),
        cost_estimate=pl.CostEstimate(
            flops=16 * channels * width * width * blocks * blocks,
            bytes_accessed=10 * channels * blocks * width,
            transcendentals=0,
        ),
    )(taps, product, filters)


def gate_kernel(place_ref, taps_ref, q_ref, y_ref, *outs):
    blocks, channels, width = q_ref.shape
    lane = lax.broadcasted_iota(jnp.int32, (channels, width), 1)
    columns = taps_ref[...].T
    taps = [jnp.broadcast_to(columns[:, place : place + 1], lane.shape) for place in range(3)]
    inner = len(outs)
    for offset, out in enumerate(outs):
        for outer in range(blocks // inner):
            block = outer * inner + jnp.bitwise_xor(place_ref[0], offset)
            query = q_ref[block].astype(jnp.float32)
            earlier = q_ref[jnp.maximum(block - 1, 0)].astype(jnp.float32)
            earlier = jnp.where(block > 0, earlier, 0.0)
            once, twice = (
                jnp.where(lane >= steps, pltpu.roll(query, steps, 1), pltpu.roll(earlier, steps, 1))
                for steps in (1, 2)
            )
            query_short = taps[0] * query + taps[1] * once + taps[2] * twice
            gated = query_short * y_ref[pl.ds(block, channels, stride=blocks), :]
            out[outer] = gated.T.astype(out.dtype)


def gate(place, taps, query, mixed, inner):
    blocks, channels, width = query.shape
    return pl.pallas_call(
        gate_kernel,
        out_shape=[jax.ShapeDtypeStruct((blocks // inner, width, channels), jnp.bfloat16)] * inner,
        in_specs=[SMEM] + [VMEM] * 3,
        out_specs=[VMEM] * inner,
        compiler_params=pltpu.CompilerParams(vmem_limit_bytes=VMEM_LIMIT),
    )(place, taps, query, mixed)


def project_kernel(place_ref, own_ref, other_ref, *refs):
    weights, outs = refs[:-4], refs[-4:]
    planes, depth = own_ref.shape[1], own_ref.shape[3]
    inner, outer, core = place_ref[0], place_ref[1], place_ref[2]
    for out, step in zip(outs, STEPS):
        plane = (outer + step) % planes
        total = None
        for index in range(PLANE):
            if len(weights) == 1:
                owner, weight = index, weights[0][2 * depth * index : 2 * depth * (index + 1)]
            elif index + 1 < PLANE:
                owner, weight = jnp.bitwise_xor(inner, index), weights[index][...]
            else:
                owner = jnp.bitwise_xor(inner, index)
                weight = jnp.concatenate([ref[...] for ref in weights[index:]], axis=0)
            mine = jnp.bitwise_xor(owner // 2, core) == 0
            halves = []
            for half in range(2):
                source = jnp.bitwise_xor(2 * (owner % 2) + half, inner)
                halves.append(jnp.where(mine, own_ref[source, plane], other_ref[source, plane]))
            term = jnp.dot(
                jnp.concatenate(halves, axis=1), weight, preferred_element_type=jnp.float32
            )
            total = term if total is None else total + term
        out[...] = total.astype(out.dtype)


STEPS = (2, 1, 3, 0)


def project(place, gates, weights, columns):
    _, _, rows, _ = gates[0].shape
    specs = [
        pl.BlockSpec(
            (weight.shape[0], columns),
            functools.partial(lambda block, step, place_ref: (0, block), first // columns),
        )
        for weight, first in weights
    ]
    whole = pl.BlockSpec(gates[0].shape, lambda step, place_ref: (0,) * 4)
    kinds = [jnp.bfloat16] * 3 + [jnp.float32]
    return pl.pallas_call(
        project_kernel,
        out_shape=[jax.ShapeDtypeStruct((rows, columns), kind) for kind in kinds],
        grid_spec=pltpu.PrefetchScalarGridSpec(
            num_scalar_prefetch=1,
            grid=(1,),
            in_specs=[whole] * 2 + specs,
            out_specs=[pl.BlockSpec((rows, columns), lambda step, place_ref: (0, 0))] * 4,
        ),
        compiler_params=pltpu.CompilerParams(vmem_limit_bytes=VMEM_LIMIT),
        cost_estimate=pl.CostEstimate(flops=rows * columns, bytes_accessed=0, transcendentals=0),
    )(place, *gates, *[weight for weight, _ in weights])


def by_planes(query_proj, key_proj, value_proj, short_taps, long_filters, out_weight):
    seq_count, tp_count = lax.axis_size("seq"), lax.axis_size("tp")
    planes = seq_count // PLANE
    place_seq, core = lax.axis_index("seq"), lax.axis_index("tp")
    place = jnp.stack([place_seq % PLANE, place_seq // PLANE, core]).astype(jnp.int32)
    channels, width = long_filters.shape[0], query_proj.shape[1]

    across = [(source, source ^ 1) for source in range(seq_count)]
    along = [(source, source ^ 2) for source in range(seq_count)]
    up = [(source, (source + PLANE) % seq_count) for source in range(seq_count)]
    down = [(target, source) for source, target in up]

    def to_plane_of_rows(message, offset):
        pairs = []
        for source in range(seq_count):
            z, q = divmod(source, PLANE)
            for tp in range(tp_count):
                target = (planes // tp_count * tp + z // tp_count) * PLANE + (q ^ offset)
                pairs.append((source * tp_count + tp, target * tp_count + z % tp_count))
        return lax.ppermute(message, ("seq", "tp"), pairs)

    def from_neighbours(first, count):
        part = out_weight[:, first : first + count]
        return [part, lax.ppermute(part, "seq", across), lax.ppermute(part, "seq", along)]

    def from_corner(part, from_x, from_y, first, count):
        half = part.shape[0] // 2
        top = lax.ppermute(from_y[:half, first : first + count], "seq", across)
        end = lax.ppermute(from_x[half:, first : first + count], "seq", along)
        return [(part, first), (from_x, first), (from_y, first), (top, 0), (end, 0)]

    spans, first = [], 0
    for share in COLUMN_SHARES:
        count = out_weight.shape[1] * share // sum(COLUMN_SHARES)
        spans.append((first, count))
        first += count

    groups = [list(range(first, first + PLANE)) for first in range(0, seq_count, PLANE)]
    early = out_weight[:, : spans[0][1]]
    early = lax.all_gather(early, "seq", axis=0, tiled=True, axis_index_groups=groups)
    half = spans[0][1] // 2
    halves = [([(early, 0)], half), ([(early, half)], half)]
    taps = jnp.pad(
        short_taps.reshape(-1, short_taps.shape[2]),
        ((0, EDGE_ROWS - short_taps.shape[0] * short_taps.shape[1]), (0, 0)),
    )
    product = gated_product(taps, key_proj, value_proj)
    spread = lax.all_to_all(product, "seq", split_axis=0, concat_axis=0, tiled=True)
    taps_here = lax.dynamic_slice_in_dim(taps, place_seq * channels, channels, axis=1)
    spread, query_proj = lax.optimization_barrier((spread, query_proj))
    query = lax.all_to_all(
        query_proj.reshape(seq_count, channels, width), "seq", split_axis=0, concat_axis=0, tiled=True
    )
    mixed = convolve(taps_here, spread, long_filters)
    landed = [
        to_plane_of_rows(message, offset)
        for offset, message in enumerate(gate(place, taps_here, query, mixed, PLANE))
    ]
    landed[0], out_weight = lax.optimization_barrier((landed[0], out_weight))
    late = from_neighbours(*spans[1])
    own = jnp.stack(landed)
    gates = [own, lax.ppermute(own, "tp", [(0, 1), (1, 0)])]

    parts, sums, sent = [], [], []
    for index in range(4):
        if index == 2:
            sent += [lax.ppermute(sums[0], "seq", up), lax.ppermute(sums[1], "seq", down)]
            late, sums[0] = lax.optimization_barrier((late, sums[0]))
            half = spans[1][1] // 2
            halves += [(from_corner(*late, first, half), half) for first in (0, half)]
            gates, parts, sums = lax.optimization_barrier((gates, parts, sums))
        elif index == 3:
            gates, sent = lax.optimization_barrier((gates, sent))
        weights, count = halves[index]
        forth, back = (up, down) if index % 2 == 0 else (down, up)
        far, ahead, behind, mine = project(place, gates, weights, count)
        if index % 2 == 1:
            ahead, behind = behind, ahead
        far = lax.ppermute(far, "seq", forth)
        near = lax.ppermute(behind, "seq", back)
        sums.append((ahead.astype(jnp.float32) + far.astype(jnp.float32)).astype(jnp.bfloat16))
        parts.append(mine + near.astype(jnp.float32))
    sent += [lax.ppermute(sums[-2], "seq", up), lax.ppermute(sums[-1], "seq", down)]
    columns = [part + value.astype(jnp.float32) for part, value in zip(parts, sent)]
    return jnp.concatenate(columns, axis=1).astype(jnp.bfloat16)


PRECISE = lax.Precision.HIGHEST


def phase_table(period, out_size, in_size, direction):
    out_index = lax.broadcasted_iota(jnp.int32, (out_size, in_size), 0)
    in_index = lax.broadcasted_iota(jnp.int32, (out_size, in_size), 1)
    phase_angle = (out_index * in_index % period).astype(jnp.float32) * (
        direction * 2.0 * math.pi / period
    )
    return (jnp.cos(phase_angle), jnp.sin(phase_angle))


def left_apply(phase, signal):
    return jnp.einsum("kn,cnm->ckm", phase, signal, precision=PRECISE)


def right_apply(signal, phase):
    return jnp.einsum("ckn,nm->ckm", signal, phase, precision=PRECISE)


def forward_spectrum(signal, inner_size):
    channels_here, length = signal.shape
    period = 2 * length
    outer_size = period // inner_size
    blocks = signal.reshape(channels_here, outer_size // 2, inner_size)
    left_re, left_im = phase_table(outer_size, outer_size, outer_size // 2, -1.0)
    section_re = left_apply(left_re, blocks)
    section_im = left_apply(left_im, blocks)
    twist_re, twist_im = phase_table(period, outer_size, inner_size, -1.0)
    turned_re = section_re * twist_re - section_im * twist_im
    turned_im = section_re * twist_im + section_im * twist_re
    right_re, right_im = phase_table(inner_size, inner_size, inner_size, -1.0)
    spec_re = right_apply(turned_re, right_re) - right_apply(turned_im, right_im)
    spec_im = right_apply(turned_re, right_im) + right_apply(turned_im, right_re)
    return (spec_re, spec_im)


def inverse_signal(spec_re, spec_im, length, inner_size):
    channels_here = spec_re.shape[0]
    period = 2 * length
    outer_size = period // inner_size
    right_re, right_im = phase_table(inner_size, inner_size, inner_size, 1.0)
    mid_re = right_apply(spec_re, right_re) - right_apply(spec_im, right_im)
    mid_im = right_apply(spec_re, right_im) + right_apply(spec_im, right_re)
    twist_re, twist_im = phase_table(period, outer_size, inner_size, 1.0)
    turned_re = mid_re * twist_re - mid_im * twist_im
    turned_im = mid_re * twist_im + mid_im * twist_re
    left_re, left_im = phase_table(outer_size, outer_size // 2, outer_size, 1.0)
    signal = left_apply(left_re, turned_re) - left_apply(left_im, turned_im)
    return signal.reshape(channels_here, length) / period


def long_convolve(signal, filters, inner_size):
    length = signal.shape[1]
    data_re, data_im = forward_spectrum(signal, inner_size)
    filt_re, filt_im = forward_spectrum(filters, inner_size)
    prod_re = data_re * filt_re - data_im * filt_im
    prod_im = data_re * filt_im + data_im * filt_re
    return inverse_signal(prod_re, prod_im, length, inner_size)


def by_whole_rows(query_proj, key_proj, value_proj, short_taps, long_filters, out_weight):
    inner_size = query_proj.shape[1] // 2
    query_short, key_short, value_short = filtered_streams(
        (query_proj, key_proj, value_proj), short_taps
    )
    product = (key_short * value_short).astype(jnp.bfloat16)
    spread = lax.all_to_all(product, "seq", split_axis=0, concat_axis=1, tiled=True)
    mixed_conv = long_convolve(spread.astype(jnp.float32), long_filters, inner_size)
    returned = lax.all_to_all(mixed_conv, "seq", split_axis=1, concat_axis=0, tiled=True)
    gated_out = (query_short * returned).astype(jnp.bfloat16)
    result = lax.dot_general(
        lax.all_gather(gated_out, "tp", axis=0, tiled=True),
        lax.all_gather(out_weight, "seq", axis=0, tiled=True),
        (((0,), (0,)), ((), ())),
        preferred_element_type=jnp.float32,
    )
    return result.astype(jnp.bfloat16)


def solution(mesh):
    planes, cores = mesh.shape["seq"] // PLANE, mesh.shape["tp"]
    plan = by_planes if planes == PLANE and cores == 2 else by_whole_rows
    return jax.shard_map(
        plan,
        mesh=mesh,
        in_specs=(
            P("tp", "seq"),
            P("tp", "seq"),
            P("tp", "seq"),
            P(None, None, "tp"),
            P(("tp", "seq"), None),
            P("seq", "tp"),
        ),
        out_specs=P("seq", "tp"),
        check_vma=False,
    )
```

```python
import functools
import math

import jax
import jax.numpy as jnp
from jax import lax
from jax.experimental import pallas as pl
from jax.experimental.pallas import tpu as pltpu
from jax.sharding import PartitionSpec as P

COLUMN_SHARES = (14, 18)
PLANE = 4
VMEM_LIMIT = 16 * 2**20


def shifted(value, axis, steps):
    count = lax.axis_size(axis)
    initial, last = (max(0, -steps), min(count, count - steps))
    return lax.ppermute(value, axis, [(source, source + steps) for source in range(initial, last)])


def short_filter(extended, tap_weights):
    return (
        tap_weights[0][:, None] * extended[:, 2:]
        + tap_weights[1][:, None] * extended[:, 1:-1]
        + tap_weights[2][:, None] * extended[:, :-2]
    )


def filtered_streams(streams, taps):
    before = shifted(jnp.stack([stream[:, -2:] for stream in streams]), "seq", 1)
    extended = [
        jnp.concatenate([before[index], stream], axis=1).astype(jnp.float32)
        for index, stream in enumerate(streams)
    ]
    return [short_filter(value, tap) for value, tap in zip(extended, taps)]


VMEM = pl.BlockSpec(memory_space=pltpu.VMEM)
SMEM = pl.BlockSpec(memory_space=pltpu.SMEM)
EDGE_ROWS = 16


def picked_rows(stream, pairs):
    width = stream.shape[1]
    row = lax.broadcasted_iota(jnp.int32, (EDGE_ROWS, width), 0)
    lane = lax.broadcasted_iota(jnp.int32, (EDGE_ROWS, width), 1)
    picked = functools.reduce(
        jnp.logical_or, [(row == out) & (lane == position) for out, position in pairs]
    )
    return lax.dot_general(
        jnp.where(picked, 1.0, 0.0).astype(stream.dtype),
        stream,
        (((1,), (1,)), ((), ())),
        preferred_element_type=jnp.float32,
    )


def moved_rows(stream):
    width = stream.shape[1]
    row = lax.broadcasted_iota(jnp.int32, (3 * width, width), 0)
    lane = lax.broadcasted_iota(jnp.int32, (3 * width, width), 1)
    picked = jnp.where(lane == row % width - row // width, 1.0, 0.0).astype(stream.dtype)
    moved = lax.dot_general(
        picked, stream, (((1,), (1,)), ((), ())), preferred_element_type=jnp.float32
    )
    return moved[:width], moved[width : 2 * width], moved[2 * width :]


def short_filtered(stream, index, taps_ref, spot):
    now, once, twice = moved_rows(stream)
    tap = lambda place: taps_ref[3 * index + place : 3 * index + place + 1, spot]
    return tap(0) * now + tap(1) * once + tap(2) * twice


def product_kernel(taps_ref, key_ref, value_ref, out_ref):
    blocks, rows, width = out_ref.shape
    for block in range(blocks):
        spot = pl.ds(block * width, width)
        key, value = key_ref[spot], value_ref[spot]
        product = short_filtered(key, 1, taps_ref, spot)
        product = product * short_filtered(value, 2, taps_ref, spot)
        out_ref[block, :width] = product.T.astype(out_ref.dtype)
        places = (0, 1, width - 2, width - 1)
        edges = picked_rows(key, list(enumerate(places)))
        edges = edges + picked_rows(value, [(4 + out, place) for out, place in enumerate(places)])
        out_ref[block, width:] = edges.astype(out_ref.dtype)


def gated_product(taps, key, value):
    channels, width = key.shape
    return pl.pallas_call(
        product_kernel,
        out_shape=jax.ShapeDtypeStruct((channels // width, width + EDGE_ROWS, width), key.dtype),
        in_specs=[VMEM] * 3,
        out_specs=VMEM,
        compiler_params=pltpu.CompilerParams(vmem_limit_bytes=VMEM_LIMIT),
    )(taps, key, value)


def first_products(taps, edges, earlier):
    short = []
    for stream in range(2):
        tap = [taps[3 * (stream + 1) + place : 3 * (stream + 1) + place + 1] for place in range(3)]
        start, then = (edges[4 * stream + place : 4 * stream + place + 1] for place in range(2))
        second, first = (earlier[4 * stream + place : 4 * stream + place + 1] for place in (2, 3))
        short.append(
            (
                tap[0] * start + tap[1] * first + tap[2] * second,
                tap[0] * then + tap[1] * start + tap[2] * first,
            )
        )
    return [(key * value).astype(jnp.bfloat16).astype(jnp.float32) for key, value in zip(*short)]


BAND = 64
GROUP = 16


def conv_kernel(taps_ref, x_ref, h_ref, result, signals_f32, turned_filters, shifted_x):
    blocks, width = x_ref.shape[0], x_ref.shape[2]
    channels = h_ref.shape[0]
    parts = width // BAND
    band_lane = lax.broadcasted_iota(jnp.int32, (BAND, width), 1)
    keep = band_lane > lax.broadcasted_iota(jnp.int32, (BAND, width), 0)
    lane = lax.broadcasted_iota(jnp.int32, (blocks, width), 1)
    row = lax.broadcasted_iota(jnp.int32, (blocks, width), 0)
    square_row = lax.broadcasted_iota(jnp.int32, (width, width), 0)
    square_lane = lax.broadcasted_iota(jnp.int32, (width, width), 1)
    exchange = jnp.where(square_row + square_lane == width - 1, 1.0, 0.0).astype(jnp.bfloat16)
    shifted_x[...] = jnp.zeros(shifted_x.shape, jnp.float32)
    tile_lane = lax.broadcasted_iota(jnp.int32, (channels, width), 1)
    taps = taps_ref[...]
    earlier_edges = jnp.zeros((EDGE_ROWS, channels), jnp.float32)
    for block in range(blocks):
        edges = x_ref[block, channels:].astype(jnp.float32)
        pair = first_products(taps, edges, earlier_edges)
        earlier_edges = edges
        pair_row = lax.broadcasted_iota(jnp.int32, (8, channels), 0)
        pair = jnp.where(pair_row == 0, pair[0], jnp.where(pair_row == 1, pair[1], 0.0)).T
        tile = x_ref[block, :channels].astype(jnp.float32)
        tile = jnp.where(tile_lane == 0, pair[:, :1], jnp.where(tile_lane == 1, pair[:, 1:2], tile))
        signals_f32[block * channels : (block + 1) * channels] = tile
        turned_filters[blocks - 1 - block] = jnp.dot(
            h_ref[:, block * width : (block + 1) * width].astype(jnp.bfloat16),
            exchange,
            preferred_element_type=jnp.float32,
        )

    def one_channel(slot, channel):
        signal = signals_f32[pl.ds(channel, blocks, stride=channels), :]
        shifted_x[slot, 0, blocks : 2 * blocks] = signal
        for part in range(1, parts):
            left = width - BAND * part
            turned = pltpu.roll(signal, left, 1)
            following = jnp.where(row == blocks - 1, 0.0, pltpu.roll(turned, blocks - 1, 0))
            shifted_x[slot, part, blocks : 2 * blocks] = jnp.where(lane < left, turned, following)
            shifted_x[slot, part, blocks - 8 : blocks] = jnp.where(
                (lane[:8] >= left) & (row[:8] == 7), jnp.broadcast_to(turned[:1], (8, width)), 0.0
            )
        earlier = jnp.zeros((BAND, width), jnp.float32)
        bands, signals = [], []
        for lag in range(blocks + 1):
            delayed_filter = jnp.zeros((BAND, width), jnp.float32)
            if lag < blocks:
                delayed_filter = pltpu.roll(
                    jnp.broadcast_to(turned_filters[lag, pl.ds(channel, 1), :], (BAND, width)),
                    1,
                    1,
                    stride=1,
                    stride_axis=0,
                )
            bands.append(jnp.where(keep, delayed_filter, earlier).astype(jnp.bfloat16))
            earlier = delayed_filter
            ahead = [shifted_x[slot, part, lag : lag + blocks, :] for part in range(parts)]
            signals.append(jnp.concatenate(ahead, axis=0).astype(jnp.bfloat16))
        total = lax.dot_general(
            jnp.concatenate(signals, axis=1),
            jnp.concatenate(bands, axis=1),
            (((1,), (1,)), ((), ())),
            preferred_element_type=jnp.float32,
        )
        result[pl.ds(pl.multiple_of(channel * blocks, blocks), blocks), :] = jnp.concatenate(
            [total[part * blocks : (part + 1) * blocks] for part in range(parts)], axis=1
        )

    def one_group(group, carry):
        for slot in range(GROUP):
            one_channel(slot, group * GROUP + slot)
        return carry

    lax.fori_loop(0, channels // GROUP, one_group, 0)


def convolve(taps, product, filters):
    blocks, _, width = product.shape
    channels = filters.shape[0]
    return pl.pallas_call(
        conv_kernel,
        out_shape=jax.ShapeDtypeStruct(((channels + 1) * blocks, width), jnp.float32),
        in_specs=[VMEM] * 3,
        out_specs=VMEM,
        scratch_shapes=[
            pltpu.VMEM(((blocks + 1) * channels, width), jnp.float32),
            pltpu.VMEM((blocks, channels, width), jnp.float32),
            pltpu.VMEM((GROUP, width // BAND, 2 * blocks + 8, width), jnp.float32),
        ],
        compiler_params=pltpu.CompilerParams(vmem_limit_bytes=VMEM_LIMIT),
        cost_estimate=pl.CostEstimate(
            flops=16 * channels * width * width * blocks * blocks,
            bytes_accessed=10 * channels * blocks * width,
            transcendentals=0,
        ),
    )(taps, product, filters)


def gate_kernel(place_ref, taps_ref, q_ref, y_ref, *outs):
    blocks, channels, width = q_ref.shape
    lane = lax.broadcasted_iota(jnp.int32, (channels, width), 1)
    columns = taps_ref[...].T
    taps = [jnp.broadcast_to(columns[:, place : place + 1], lane.shape) for place in range(3)]
    inner = len(outs)
    for offset, out in enumerate(outs):
        for outer in range(blocks // inner):
            block = outer * inner + jnp.bitwise_xor(place_ref[0], offset)
            query = q_ref[block].astype(jnp.float32)
            earlier = q_ref[jnp.maximum(block - 1, 0)].astype(jnp.float32)
            earlier = jnp.where(block > 0, earlier, 0.0)
            once, twice = (
                jnp.where(lane >= steps, pltpu.roll(query, steps, 1), pltpu.roll(earlier, steps, 1))
                for steps in (1, 2)
            )
            query_short = taps[0] * query + taps[1] * once + taps[2] * twice
            gated = query_short * y_ref[pl.ds(block, channels, stride=blocks), :]
            out[outer] = gated.T.astype(out.dtype)


def gate(place, taps, query, mixed, inner):
    blocks, channels, width = query.shape
    return pl.pallas_call(
        gate_kernel,
        out_shape=[jax.ShapeDtypeStruct((blocks // inner, width, channels), jnp.bfloat16)] * inner,
        in_specs=[SMEM] + [VMEM] * 3,
        out_specs=[VMEM] * inner,
        compiler_params=pltpu.CompilerParams(vmem_limit_bytes=VMEM_LIMIT),
    )(place, taps, query, mixed)


def project_kernel(place_ref, own_ref, other_ref, *refs):
    weights, outs = refs[:-4], refs[-4:]
    planes, depth = own_ref.shape[1], own_ref.shape[3]
    inner, outer, core = place_ref[0], place_ref[1], place_ref[2]
    for out, step in zip(outs, STEPS):
        plane = (outer + step) % planes
        total = None
        for index in range(PLANE):
            if len(weights) == 1:
                owner, weight = index, weights[0][2 * depth * index : 2 * depth * (index + 1)]
            elif index + 1 < PLANE:
                owner, weight = jnp.bitwise_xor(inner, index), weights[index][...]
            else:
                owner = jnp.bitwise_xor(inner, index)
                weight = jnp.concatenate([ref[...] for ref in weights[index:]], axis=0)
            mine = jnp.bitwise_xor(owner // 2, core) == 0
            halves = []
            for half in range(2):
                source = jnp.bitwise_xor(2 * (owner % 2) + half, inner)
                halves.append(jnp.where(mine, own_ref[source, plane], other_ref[source, plane]))
            term = jnp.dot(
                jnp.concatenate(halves, axis=1), weight, preferred_element_type=jnp.float32
            )
            total = term if total is None else total + term
        out[...] = total.astype(out.dtype)


STEPS = (2, 1, 3, 0)


def project(place, gates, weights, columns):
    _, _, rows, _ = gates[0].shape
    specs = [
        pl.BlockSpec(
            (weight.shape[0], columns),
            functools.partial(lambda block, step, place_ref: (0, block), first // columns),
        )
        for weight, first in weights
    ]
    whole = pl.BlockSpec(gates[0].shape, lambda step, place_ref: (0,) * 4)
    kinds = [jnp.bfloat16] * 3 + [jnp.float32]
    return pl.pallas_call(
        project_kernel,
        out_shape=[jax.ShapeDtypeStruct((rows, columns), kind) for kind in kinds],
        grid_spec=pltpu.PrefetchScalarGridSpec(
            num_scalar_prefetch=1,
            grid=(1,),
            in_specs=[whole] * 2 + specs,
            out_specs=[pl.BlockSpec((rows, columns), lambda step, place_ref: (0, 0))] * 4,
        ),
        compiler_params=pltpu.CompilerParams(vmem_limit_bytes=VMEM_LIMIT),
        cost_estimate=pl.CostEstimate(flops=rows * columns, bytes_accessed=0, transcendentals=0),
    )(place, *gates, *[weight for weight, _ in weights])


def by_planes(query_proj, key_proj, value_proj, short_taps, long_filters, out_weight):
    seq_count, tp_count = lax.axis_size("seq"), lax.axis_size("tp")
    planes = seq_count // PLANE
    place_seq, core = lax.axis_index("seq"), lax.axis_index("tp")
    place = jnp.stack([place_seq % PLANE, place_seq // PLANE, core]).astype(jnp.int32)
    channels, width = long_filters.shape[0], query_proj.shape[1]

    across = [(source, source ^ 1) for source in range(seq_count)]
    along = [(source, source ^ 2) for source in range(seq_count)]
    up = [(source, (source + PLANE) % seq_count) for source in range(seq_count)]
    down = [(target, source) for source, target in up]

    def to_plane_of_rows(message, offset):
        pairs = []
        for source in range(seq_count):
            z, q = divmod(source, PLANE)
            for tp in range(tp_count):
                target = (planes // tp_count * tp + z // tp_count) * PLANE + (q ^ offset)
                pairs.append((source * tp_count + tp, target * tp_count + z % tp_count))
        return lax.ppermute(message, ("seq", "tp"), pairs)

    def from_neighbours(first, count):
        part = out_weight[:, first : first + count]
        return [part, lax.ppermute(part, "seq", across), lax.ppermute(part, "seq", along)]

    def from_corner(part, from_x, from_y, first, count):
        half = part.shape[0] // 2
        top = lax.ppermute(from_y[:half, first : first + count], "seq", across)
        end = lax.ppermute(from_x[half:, first : first + count], "seq", along)
        return [(part, first), (from_x, first), (from_y, first), (top, 0), (end, 0)]

    spans, first = [], 0
    for share in COLUMN_SHARES:
        count = out_weight.shape[1] * share // sum(COLUMN_SHARES)
        spans.append((first, count))
        first += count

    groups = [list(range(first, first + PLANE)) for first in range(0, seq_count, PLANE)]
    early = out_weight[:, : spans[0][1]]
    early = lax.all_gather(early, "seq", axis=0, tiled=True, axis_index_groups=groups)
    half = spans[0][1] // 2
    halves = [([(early, 0)], half), ([(early, half)], half)]
    taps = jnp.pad(
        short_taps.reshape(-1, short_taps.shape[2]),
        ((0, EDGE_ROWS - short_taps.shape[0] * short_taps.shape[1]), (0, 0)),
    )
    product = gated_product(taps, key_proj, value_proj)
    spread = lax.all_to_all(product, "seq", split_axis=0, concat_axis=0, tiled=True)
    taps_here = lax.dynamic_slice_in_dim(taps, place_seq * channels, channels, axis=1)
    spread, query_proj = lax.optimization_barrier((spread, query_proj))
    query = lax.all_to_all(
        query_proj.reshape(seq_count, channels, width), "seq", split_axis=0, concat_axis=0, tiled=True
    )
    mixed = convolve(taps_here, spread, long_filters)
    landed = [
        to_plane_of_rows(message, offset)
        for offset, message in enumerate(gate(place, taps_here, query, mixed, PLANE))
    ]
    landed[0], out_weight = lax.optimization_barrier((landed[0], out_weight))
    late = from_neighbours(*spans[1])
    own = jnp.stack(landed)
    gates = [own, lax.ppermute(own, "tp", [(0, 1), (1, 0)])]

    parts, sums, sent = [], [], []
    for index in range(4):
        if index == 2:
            sent += [lax.ppermute(sums[0], "seq", up), lax.ppermute(sums[1], "seq", down)]
            late, sums[0] = lax.optimization_barrier((late, sums[0]))
            half = spans[1][1] // 2
            halves += [(from_corner(*late, first, half), half) for first in (0, half)]
            gates, parts, sums = lax.optimization_barrier((gates, parts, sums))
        elif index == 3:
            gates, sent = lax.optimization_barrier((gates, sent))
        weights, count = halves[index]
        forth, back = (up, down) if index % 2 == 0 else (down, up)
        far, ahead, behind, mine = project(place, gates, weights, count)
        if index % 2 == 1:
            ahead, behind = behind, ahead
        far = lax.ppermute(far, "seq", forth)
        near = lax.ppermute(behind, "seq", back)
        sums.append((ahead.astype(jnp.float32) + far.astype(jnp.float32)).astype(jnp.bfloat16))
        parts.append(mine + near.astype(jnp.float32))
    sent += [lax.ppermute(sums[-2], "seq", up), lax.ppermute(sums[-1], "seq", down)]
    columns = [part + value.astype(jnp.float32) for part, value in zip(parts, sent)]
    return jnp.concatenate(columns, axis=1).astype(jnp.bfloat16)


PRECISE = lax.Precision.HIGHEST


def phase_table(period, out_size, in_size, direction):
    out_index = lax.broadcasted_iota(jnp.int32, (out_size, in_size), 0)
    in_index = lax.broadcasted_iota(jnp.int32, (out_size, in_size), 1)
    phase_angle = (out_index * in_index % period).astype(jnp.float32) * (
        direction * 2.0 * math.pi / period
    )
    return (jnp.cos(phase_angle), jnp.sin(phase_angle))


def left_apply(phase, signal):
    return jnp.einsum("kn,cnm->ckm", phase, signal, precision=PRECISE)


def right_apply(signal, phase):
    return jnp.einsum("ckn,nm->ckm", signal, phase, precision=PRECISE)


def forward_spectrum(signal, inner_size):
    channels_here, length = signal.shape
    period = 2 * length
    outer_size = period // inner_size
    blocks = signal.reshape(channels_here, outer_size // 2, inner_size)
    left_re, left_im = phase_table(outer_size, outer_size, outer_size // 2, -1.0)
    section_re = left_apply(left_re, blocks)
    section_im = left_apply(left_im, blocks)
    twist_re, twist_im = phase_table(period, outer_size, inner_size, -1.0)
    turned_re = section_re * twist_re - section_im * twist_im
    turned_im = section_re * twist_im + section_im * twist_re
    right_re, right_im = phase_table(inner_size, inner_size, inner_size, -1.0)
    spec_re = right_apply(turned_re, right_re) - right_apply(turned_im, right_im)
    spec_im = right_apply(turned_re, right_im) + right_apply(turned_im, right_re)
    return (spec_re, spec_im)


def inverse_signal(spec_re, spec_im, length, inner_size):
    channels_here = spec_re.shape[0]
    period = 2 * length
    outer_size = period // inner_size
    right_re, right_im = phase_table(inner_size, inner_size, inner_size, 1.0)
    mid_re = right_apply(spec_re, right_re) - right_apply(spec_im, right_im)
    mid_im = right_apply(spec_re, right_im) + right_apply(spec_im, right_re)
    twist_re, twist_im = phase_table(period, outer_size, inner_size, 1.0)
    turned_re = mid_re * twist_re - mid_im * twist_im
    turned_im = mid_re * twist_im + mid_im * twist_re
    left_re, left_im = phase_table(outer_size, outer_size // 2, outer_size, 1.0)
    signal = left_apply(left_re, turned_re) - left_apply(left_im, turned_im)
    return signal.reshape(channels_here, length) / period


def long_convolve(signal, filters, inner_size):
    length = signal.shape[1]
    data_re, data_im = forward_spectrum(signal, inner_size)
    filt_re, filt_im = forward_spectrum(filters, inner_size)
    prod_re = data_re * filt_re - data_im * filt_im
    prod_im = data_re * filt_im + data_im * filt_re
    return inverse_signal(prod_re, prod_im, length, inner_size)


def by_whole_rows(query_proj, key_proj, value_proj, short_taps, long_filters, out_weight):
    inner_size = query_proj.shape[1] // 2
    query_short, key_short, value_short = filtered_streams(
        (query_proj, key_proj, value_proj), short_taps
    )
    product = (key_short * value_short).astype(jnp.bfloat16)
    spread = lax.all_to_all(product, "seq", split_axis=0, concat_axis=1, tiled=True)
    mixed_conv = long_convolve(spread.astype(jnp.float32), long_filters, inner_size)
    returned = lax.all_to_all(mixed_conv, "seq", split_axis=1, concat_axis=0, tiled=True)
    gated_out = (query_short * returned).astype(jnp.bfloat16)
    result = lax.dot_general(
        lax.all_gather(gated_out, "tp", axis=0, tiled=True),
        lax.all_gather(out_weight, "seq", axis=0, tiled=True),
        (((0,), (0,)), ((), ())),
        preferred_element_type=jnp.float32,
    )
    return result.astype(jnp.bfloat16)


def solution(mesh):
    planes, cores = mesh.shape["seq"] // PLANE, mesh.shape["tp"]
    plan = by_planes if planes == PLANE and cores == 2 else by_whole_rows
    return jax.shard_map(
        plan,
        mesh=mesh,
        in_specs=(
            P("tp", "seq"),
            P("tp", "seq"),
            P("tp", "seq"),
            P(None, None, "tp"),
            P(("tp", "seq"), None),
            P("seq", "tp"),
        ),
        out_specs=P("seq", "tp"),
        check_vma=False,
    )
```

```python
import functools
import math

import jax
import jax.numpy as jnp
from jax import lax
from jax.experimental import pallas as pl
from jax.experimental.pallas import tpu as pltpu
from jax.sharding import PartitionSpec as P

COLUMN_SHARES = (14, 18)
PLANE = 4
VMEM_LIMIT = 16 * 2**20


def shifted(value, axis, steps):
    count = lax.axis_size(axis)
    initial, last = (max(0, -steps), min(count, count - steps))
    return lax.ppermute(value, axis, [(source, source + steps) for source in range(initial, last)])


def short_filter(extended, tap_weights):
    return (
        tap_weights[0][:, None] * extended[:, 2:]
        + tap_weights[1][:, None] * extended[:, 1:-1]
        + tap_weights[2][:, None] * extended[:, :-2]
    )


def filtered_streams(streams, taps):
    before = shifted(jnp.stack([stream[:, -2:] for stream in streams]), "seq", 1)
    extended = [
        jnp.concatenate([before[index], stream], axis=1).astype(jnp.float32)
        for index, stream in enumerate(streams)
    ]
    return [short_filter(value, tap) for value, tap in zip(extended, taps)]


VMEM = pl.BlockSpec(memory_space=pltpu.VMEM)
SMEM = pl.BlockSpec(memory_space=pltpu.SMEM)
EDGE_ROWS = 16


def picked_rows(stream, pairs):
    width = stream.shape[1]
    row = lax.broadcasted_iota(jnp.int32, (EDGE_ROWS, width), 0)
    lane = lax.broadcasted_iota(jnp.int32, (EDGE_ROWS, width), 1)
    picked = functools.reduce(
        jnp.logical_or, [(row == out) & (lane == position) for out, position in pairs]
    )
    return lax.dot_general(
        jnp.where(picked, 1.0, 0.0).astype(stream.dtype),
        stream,
        (((1,), (1,)), ((), ())),
        preferred_element_type=jnp.float32,
    )


def moved_rows(stream):
    width = stream.shape[1]
    row = lax.broadcasted_iota(jnp.int32, (3 * width, width), 0)
    lane = lax.broadcasted_iota(jnp.int32, (3 * width, width), 1)
    picked = jnp.where(lane == row % width - row // width, 1.0, 0.0).astype(stream.dtype)
    moved = lax.dot_general(
        picked, stream, (((1,), (1,)), ((), ())), preferred_element_type=jnp.float32
    )
    return moved[:width], moved[width : 2 * width], moved[2 * width :]


def short_filtered(stream, index, taps_ref, spot):
    now, once, twice = moved_rows(stream)
    tap = lambda place: taps_ref[3 * index + place : 3 * index + place + 1, spot]
    return tap(0) * now + tap(1) * once + tap(2) * twice


def product_kernel(taps_ref, key_ref, value_ref, out_ref):
    blocks, rows, width = out_ref.shape
    for block in range(blocks):
        spot = pl.ds(block * width, width)
        key, value = key_ref[spot], value_ref[spot]
        product = short_filtered(key, 1, taps_ref, spot)
        product = product * short_filtered(value, 2, taps_ref, spot)
        out_ref[block, :width] = product.T.astype(out_ref.dtype)
        places = (0, 1, width - 2, width - 1)
        edges = picked_rows(key, list(enumerate(places)))
        edges = edges + picked_rows(value, [(4 + out, place) for out, place in enumerate(places)])
        out_ref[block, width:] = edges.astype(out_ref.dtype)


def gated_product(taps, key, value):
    channels, width = key.shape
    return pl.pallas_call(
        product_kernel,
        out_shape=jax.ShapeDtypeStruct((channels // width, width + EDGE_ROWS, width), key.dtype),
        in_specs=[VMEM] * 3,
        out_specs=VMEM,
        compiler_params=pltpu.CompilerParams(vmem_limit_bytes=VMEM_LIMIT),
    )(taps, key, value)


def first_products(taps, edges, earlier):
    short = []
    for stream in range(2):
        tap = [taps[3 * (stream + 1) + place : 3 * (stream + 1) + place + 1] for place in range(3)]
        start, then = (edges[4 * stream + place : 4 * stream + place + 1] for place in range(2))
        second, first = (earlier[4 * stream + place : 4 * stream + place + 1] for place in (2, 3))
        short.append(
            (
                tap[0] * start + tap[1] * first + tap[2] * second,
                tap[0] * then + tap[1] * start + tap[2] * first,
            )
        )
    return [(key * value).astype(jnp.bfloat16).astype(jnp.float32) for key, value in zip(*short)]


BAND = 64
GROUP = 16


def conv_kernel(taps_ref, x_ref, h_ref, result, signals_f32, turned_filters, shifted_x):
    blocks, width = x_ref.shape[0], x_ref.shape[2]
    channels = h_ref.shape[0]
    parts = width // BAND
    band_lane = lax.broadcasted_iota(jnp.int32, (BAND, width), 1)
    keep = band_lane > lax.broadcasted_iota(jnp.int32, (BAND, width), 0)
    lane = lax.broadcasted_iota(jnp.int32, (blocks, width), 1)
    row = lax.broadcasted_iota(jnp.int32, (blocks, width), 0)
    square_row = lax.broadcasted_iota(jnp.int32, (width, width), 0)
    square_lane = lax.broadcasted_iota(jnp.int32, (width, width), 1)
    exchange = jnp.where(square_row + square_lane == width - 1, 1.0, 0.0).astype(jnp.bfloat16)
    shifted_x[...] = jnp.zeros(shifted_x.shape, jnp.float32)
    tile_lane = lax.broadcasted_iota(jnp.int32, (channels, width), 1)
    taps = taps_ref[...]
    earlier_edges = jnp.zeros((EDGE_ROWS, channels), jnp.float32)
    for block in range(blocks):
        edges = x_ref[block, channels:].astype(jnp.float32)
        pair = first_products(taps, edges, earlier_edges)
        earlier_edges = edges
        pair_row = lax.broadcasted_iota(jnp.int32, (8, channels), 0)
        pair = jnp.where(pair_row == 0, pair[0], jnp.where(pair_row == 1, pair[1], 0.0)).T
        tile = x_ref[block, :channels].astype(jnp.float32)
        tile = jnp.where(tile_lane == 0, pair[:, :1], jnp.where(tile_lane == 1, pair[:, 1:2], tile))
        signals_f32[block * channels : (block + 1) * channels] = tile
        turned_filters[blocks - 1 - block] = jnp.dot(
            h_ref[:, block * width : (block + 1) * width].astype(jnp.bfloat16),
            exchange,
            preferred_element_type=jnp.float32,
        )

    def one_channel(slot, channel):
        signal = signals_f32[pl.ds(channel, blocks, stride=channels), :]
        shifted_x[slot, 0, blocks : 2 * blocks] = signal
        for part in range(1, parts):
            left = width - BAND * part
            turned = pltpu.roll(signal, left, 1)
            following = jnp.where(row == blocks - 1, 0.0, pltpu.roll(turned, blocks - 1, 0))
            shifted_x[slot, part, blocks : 2 * blocks] = jnp.where(lane < left, turned, following)
            shifted_x[slot, part, blocks - 8 : blocks] = jnp.where(
                (lane[:8] >= left) & (row[:8] == 7), jnp.broadcast_to(turned[:1], (8, width)), 0.0
            )
        earlier = jnp.zeros((BAND, width), jnp.float32)
        bands, signals = [], []
        for lag in range(blocks + 1):
            delayed_filter = jnp.zeros((BAND, width), jnp.float32)
            if lag < blocks:
                delayed_filter = pltpu.roll(
                    jnp.broadcast_to(turned_filters[lag, pl.ds(channel, 1), :], (BAND, width)),
                    1,
                    1,
                    stride=1,
                    stride_axis=0,
                )
            bands.append(jnp.where(keep, delayed_filter, earlier).astype(jnp.bfloat16))
            earlier = delayed_filter
            ahead = [shifted_x[slot, part, lag : lag + blocks, :] for part in range(parts)]
            signals.append(jnp.concatenate(ahead, axis=0).astype(jnp.bfloat16))
        total = lax.dot_general(
            jnp.concatenate(signals, axis=1),
            jnp.concatenate(bands, axis=1),
            (((1,), (1,)), ((), ())),
            preferred_element_type=jnp.float32,
        )
        result[pl.ds(pl.multiple_of(channel * blocks, blocks), blocks), :] = jnp.concatenate(
            [total[part * blocks : (part + 1) * blocks] for part in range(parts)], axis=1
        )

    def one_group(group, carry):
        for slot in range(GROUP):
            one_channel(slot, group * GROUP + slot)
        return carry

    lax.fori_loop(0, channels // GROUP, one_group, 0)


def convolve(taps, product, filters):
    blocks, _, width = product.shape
    channels = filters.shape[0]
    return pl.pallas_call(
        conv_kernel,
        out_shape=jax.ShapeDtypeStruct(((channels + 1) * blocks, width), jnp.float32),
        in_specs=[VMEM] * 3,
        out_specs=VMEM,
        scratch_shapes=[
            pltpu.VMEM(((blocks + 1) * channels, width), jnp.float32),
            pltpu.VMEM((blocks, channels, width), jnp.float32),
            pltpu.VMEM((GROUP, width // BAND, 2 * blocks + 8, width), jnp.float32),
        ],
        compiler_params=pltpu.CompilerParams(vmem_limit_bytes=VMEM_LIMIT),
        cost_estimate=pl.CostEstimate(
            flops=16 * channels * width * width * blocks * blocks,
            bytes_accessed=10 * channels * blocks * width,
            transcendentals=0,
        ),
    )(taps, product, filters)


def gate_kernel(place_ref, taps_ref, q_ref, y_ref, *outs):
    blocks, channels, width = q_ref.shape
    lane = lax.broadcasted_iota(jnp.int32, (channels, width), 1)
    columns = taps_ref[...].T
    taps = [jnp.broadcast_to(columns[:, place : place + 1], lane.shape) for place in range(3)]
    inner = len(outs)
    for offset, out in enumerate(outs):
        for outer in range(blocks // inner):
            block = outer * inner + jnp.bitwise_xor(place_ref[0], offset)
            query = q_ref[block].astype(jnp.float32)
            earlier = q_ref[jnp.maximum(block - 1, 0)].astype(jnp.float32)
            earlier = jnp.where(block > 0, earlier, 0.0)
            once, twice = (
                jnp.where(lane >= steps, pltpu.roll(query, steps, 1), pltpu.roll(earlier, steps, 1))
                for steps in (1, 2)
            )
            query_short = taps[0] * query + taps[1] * once + taps[2] * twice
            gated = query_short * y_ref[pl.ds(block, channels, stride=blocks), :]
            out[outer] = gated.T.astype(out.dtype)


def gate(place, taps, query, mixed, inner):
    blocks, channels, width = query.shape
    return pl.pallas_call(
        gate_kernel,
        out_shape=[jax.ShapeDtypeStruct((blocks // inner, width, channels), jnp.bfloat16)] * inner,
        in_specs=[SMEM] + [VMEM] * 3,
        out_specs=[VMEM] * inner,
        compiler_params=pltpu.CompilerParams(vmem_limit_bytes=VMEM_LIMIT),
    )(place, taps, query, mixed)


def project_kernel(place_ref, own_ref, other_ref, *refs):
    weights, outs = refs[:-4], refs[-4:]
    planes, depth = own_ref.shape[1], own_ref.shape[3]
    inner, outer, core = place_ref[0], place_ref[1], place_ref[2]
    for out, step in zip(outs, STEPS):
        plane = (outer + step) % planes
        total = None
        for index in range(PLANE):
            if len(weights) == 1:
                owner, weight = index, weights[0][2 * depth * index : 2 * depth * (index + 1)]
            elif index + 1 < PLANE:
                owner, weight = jnp.bitwise_xor(inner, index), weights[index][...]
            else:
                owner = jnp.bitwise_xor(inner, index)
                weight = jnp.concatenate([ref[...] for ref in weights[index:]], axis=0)
            mine = jnp.bitwise_xor(owner // 2, core) == 0
            halves = []
            for half in range(2):
                source = jnp.bitwise_xor(2 * (owner % 2) + half, inner)
                halves.append(jnp.where(mine, own_ref[source, plane], other_ref[source, plane]))
            term = jnp.dot(
                jnp.concatenate(halves, axis=1), weight, preferred_element_type=jnp.float32
            )
            total = term if total is None else total + term
        out[...] = total.astype(out.dtype)


STEPS = (2, 1, 3, 0)


def project(place, gates, weights, columns):
    _, _, rows, _ = gates[0].shape
    specs = [
        pl.BlockSpec(
            (weight.shape[0], columns),
            functools.partial(lambda block, step, place_ref: (0, block), first // columns),
        )
        for weight, first in weights
    ]
    whole = pl.BlockSpec(gates[0].shape, lambda step, place_ref: (0,) * 4)
    kinds = [jnp.bfloat16] * 3 + [jnp.float32]
    return pl.pallas_call(
        project_kernel,
        out_shape=[jax.ShapeDtypeStruct((rows, columns), kind) for kind in kinds],
        grid_spec=pltpu.PrefetchScalarGridSpec(
            num_scalar_prefetch=1,
            grid=(1,),
            in_specs=[whole] * 2 + specs,
            out_specs=[pl.BlockSpec((rows, columns), lambda step, place_ref: (0, 0))] * 4,
        ),
        compiler_params=pltpu.CompilerParams(vmem_limit_bytes=VMEM_LIMIT),
        cost_estimate=pl.CostEstimate(flops=rows * columns, bytes_accessed=0, transcendentals=0),
    )(place, *gates, *[weight for weight, _ in weights])


def by_planes(query_proj, key_proj, value_proj, short_taps, long_filters, out_weight):
    seq_count, tp_count = lax.axis_size("seq"), lax.axis_size("tp")
    planes = seq_count // PLANE
    place_seq, core = lax.axis_index("seq"), lax.axis_index("tp")
    place = jnp.stack([place_seq % PLANE, place_seq // PLANE, core]).astype(jnp.int32)
    channels, width = long_filters.shape[0], query_proj.shape[1]

    across = [(source, source ^ 1) for source in range(seq_count)]
    along = [(source, source ^ 2) for source in range(seq_count)]
    up = [(source, (source + PLANE) % seq_count) for source in range(seq_count)]
    down = [(target, source) for source, target in up]

    def to_plane_of_rows(message, offset):
        pairs = []
        for source in range(seq_count):
            z, q = divmod(source, PLANE)
            for tp in range(tp_count):
                target = (planes // tp_count * tp + z // tp_count) * PLANE + (q ^ offset)
                pairs.append((source * tp_count + tp, target * tp_count + z % tp_count))
        return lax.ppermute(message, ("seq", "tp"), pairs)

    def from_neighbours(first, count):
        part = out_weight[:, first : first + count]
        return [part, lax.ppermute(part, "seq", across), lax.ppermute(part, "seq", along)]

    def from_corner(part, from_x, from_y, first, count):
        half = part.shape[0] // 2
        top = lax.ppermute(from_y[:half, first : first + count], "seq", across)
        end = lax.ppermute(from_x[half:, first : first + count], "seq", along)
        return [(part, first), (from_x, first), (from_y, first), (top, 0), (end, 0)]

    spans, first = [], 0
    for share in COLUMN_SHARES:
        count = out_weight.shape[1] * share // sum(COLUMN_SHARES)
        spans.append((first, count))
        first += count

    groups = [list(range(first, first + PLANE)) for first in range(0, seq_count, PLANE)]
    early = out_weight[:, : spans[0][1]]
    early = lax.all_gather(early, "seq", axis=0, tiled=True, axis_index_groups=groups)
    half = spans[0][1] // 2
    halves = [([(early, 0)], half), ([(early, half)], half)]
    taps = jnp.pad(
        short_taps.reshape(-1, short_taps.shape[2]),
        ((0, EDGE_ROWS - short_taps.shape[0] * short_taps.shape[1]), (0, 0)),
    )
    product = gated_product(taps, key_proj, value_proj)
    spread = lax.all_to_all(product, "seq", split_axis=0, concat_axis=0, tiled=True)
    taps_here = lax.dynamic_slice_in_dim(taps, place_seq * channels, channels, axis=1)
    spread, query_proj = lax.optimization_barrier((spread, query_proj))
    query = lax.all_to_all(
        query_proj.reshape(seq_count, channels, width), "seq", split_axis=0, concat_axis=0, tiled=True
    )
    mixed = convolve(taps_here, spread, long_filters)
    landed = [
        to_plane_of_rows(message, offset)
        for offset, message in enumerate(gate(place, taps_here, query, mixed, PLANE))
    ]
    mixed, out_weight = lax.optimization_barrier((mixed, out_weight))
    late = from_neighbours(*spans[1])
    own = jnp.stack(landed)
    gates = [own, lax.ppermute(own, "tp", [(0, 1), (1, 0)])]

    parts, sums, sent = [], [], []
    for index in range(4):
        if index == 2:
            sent += [lax.ppermute(sums[0], "seq", up), lax.ppermute(sums[1], "seq", down)]
            late, sums[0] = lax.optimization_barrier((late, sums[0]))
            half = spans[1][1] // 2
            halves += [(from_corner(*late, first, half), half) for first in (0, half)]
            gates, parts, sums = lax.optimization_barrier((gates, parts, sums))
        elif index == 3:
            gates, sent = lax.optimization_barrier((gates, sent))
        weights, count = halves[index]
        forth, back = (up, down) if index % 2 == 0 else (down, up)
        far, ahead, behind, mine = project(place, gates, weights, count)
        if index % 2 == 1:
            ahead, behind = behind, ahead
        far = lax.ppermute(far, "seq", forth)
        near = lax.ppermute(behind, "seq", back)
        sums.append((ahead.astype(jnp.float32) + far.astype(jnp.float32)).astype(jnp.bfloat16))
        parts.append(mine + near.astype(jnp.float32))
    sent += [lax.ppermute(sums[-2], "seq", up), lax.ppermute(sums[-1], "seq", down)]
    columns = [part + value.astype(jnp.float32) for part, value in zip(parts, sent)]
    return jnp.concatenate(columns, axis=1).astype(jnp.bfloat16)


PRECISE = lax.Precision.HIGHEST


def phase_table(period, out_size, in_size, direction):
    out_index = lax.broadcasted_iota(jnp.int32, (out_size, in_size), 0)
    in_index = lax.broadcasted_iota(jnp.int32, (out_size, in_size), 1)
    phase_angle = (out_index * in_index % period).astype(jnp.float32) * (
        direction * 2.0 * math.pi / period
    )
    return (jnp.cos(phase_angle), jnp.sin(phase_angle))


def left_apply(phase, signal):
    return jnp.einsum("kn,cnm->ckm", phase, signal, precision=PRECISE)


def right_apply(signal, phase):
    return jnp.einsum("ckn,nm->ckm", signal, phase, precision=PRECISE)


def forward_spectrum(signal, inner_size):
    channels_here, length = signal.shape
    period = 2 * length
    outer_size = period // inner_size
    blocks = signal.reshape(channels_here, outer_size // 2, inner_size)
    left_re, left_im = phase_table(outer_size, outer_size, outer_size // 2, -1.0)
    section_re = left_apply(left_re, blocks)
    section_im = left_apply(left_im, blocks)
    twist_re, twist_im = phase_table(period, outer_size, inner_size, -1.0)
    turned_re = section_re * twist_re - section_im * twist_im
    turned_im = section_re * twist_im + section_im * twist_re
    right_re, right_im = phase_table(inner_size, inner_size, inner_size, -1.0)
    spec_re = right_apply(turned_re, right_re) - right_apply(turned_im, right_im)
    spec_im = right_apply(turned_re, right_im) + right_apply(turned_im, right_re)
    return (spec_re, spec_im)


def inverse_signal(spec_re, spec_im, length, inner_size):
    channels_here = spec_re.shape[0]
    period = 2 * length
    outer_size = period // inner_size
    right_re, right_im = phase_table(inner_size, inner_size, inner_size, 1.0)
    mid_re = right_apply(spec_re, right_re) - right_apply(spec_im, right_im)
    mid_im = right_apply(spec_re, right_im) + right_apply(spec_im, right_re)
    twist_re, twist_im = phase_table(period, outer_size, inner_size, 1.0)
    turned_re = mid_re * twist_re - mid_im * twist_im
    turned_im = mid_re * twist_im + mid_im * twist_re
    left_re, left_im = phase_table(outer_size, outer_size // 2, outer_size, 1.0)
    signal = left_apply(left_re, turned_re) - left_apply(left_im, turned_im)
    return signal.reshape(channels_here, length) / period


def long_convolve(signal, filters, inner_size):
    length = signal.shape[1]
    data_re, data_im = forward_spectrum(signal, inner_size)
    filt_re, filt_im = forward_spectrum(filters, inner_size)
    prod_re = data_re * filt_re - data_im * filt_im
    prod_im = data_re * filt_im + data_im * filt_re
    return inverse_signal(prod_re, prod_im, length, inner_size)


def by_whole_rows(query_proj, key_proj, value_proj, short_taps, long_filters, out_weight):
    inner_size = query_proj.shape[1] // 2
    query_short, key_short, value_short = filtered_streams(
        (query_proj, key_proj, value_proj), short_taps
    )
    product = (key_short * value_short).astype(jnp.bfloat16)
    spread = lax.all_to_all(product, "seq", split_axis=0, concat_axis=1, tiled=True)
    mixed_conv = long_convolve(spread.astype(jnp.float32), long_filters, inner_size)
    returned = lax.all_to_all(mixed_conv, "seq", split_axis=1, concat_axis=0, tiled=True)
    gated_out = (query_short * returned).astype(jnp.bfloat16)
    result = lax.dot_general(
        lax.all_gather(gated_out, "tp", axis=0, tiled=True),
        lax.all_gather(out_weight, "seq", axis=0, tiled=True),
        (((0,), (0,)), ((), ())),
        preferred_element_type=jnp.float32,
    )
    return result.astype(jnp.bfloat16)


def solution(mesh):
    planes, cores = mesh.shape["seq"] // PLANE, mesh.shape["tp"]
    plan = by_planes if planes == PLANE and cores == 2 else by_whole_rows
    return jax.shard_map(
        plan,
        mesh=mesh,
        in_specs=(
            P("tp", "seq"),
            P("tp", "seq"),
            P("tp", "seq"),
            P(None, None, "tp"),
            P(("tp", "seq"), None),
            P("seq", "tp"),
        ),
        out_specs=P("seq", "tp"),
        check_vma=False,
    )
```
